32 devices in a mesh: groups: 2 (over y), feat: 4 (over z), rows: 2 (over x), sub: 2 (over core).
Axes of the slice: x: 2, y: 2, z: 4, core: 2. Of those that a mesh axis runs over, the one named last changes fastest.
Arguments:
- activations: bfloat16 [8192, 28672], P(('groups', 'rows', 'sub'), 'feat'), parts along dimension 0, may hold values from -6 to 6
- out_grads: bfloat16 [8192, 8192], P(('groups', 'rows', 'sub'), 'feat'), parts along dimension 0, may hold values from -6 to 6
- proj_in: bfloat16 [57344, 128], P(('groups', 'feat')), parts along dimension 0, may hold values from -0.03125 to 0.03125
- proj_out: bfloat16 [16384, 128], P(('groups', 'feat')), parts along dimension 0, may hold values from -0.0625 to 0.0625
- lengths: int32 [256], P('groups'), parts along dimension 0, may hold values from 1 to 64, 4096 in all
- corpus: bfloat16 [16384, 16384], P(('groups', 'rows', 'sub'), 'feat'), parts along dimension 0, may hold values from -200 to 200
- owner: int32 [8192], P(('rows', 'sub')), may hold values from 0 to 255, as said below
Outputs:
- influence: float32 [256, 16384], P(('groups', 'rows', 'sub'), 'feat'), parts along dimension 0
The draws below stay inside these ranges and needn't reach their ends.
There are 2 independent parts, one for each index of `groups`. The reference program is written for one: setup_inputs(seed, part) draws one part's arguments, and reference() takes and returns one part's arrays. A program takes and returns all parts, laid end to end along the dimension named above; an argument that names none is the same for every part. Nothing has to cross between parts.
Inputs may be any that keep to these rules, and one draw needn't show every extreme that they name: `owner`: every draw holds at least two different labels, so each passage keeps some corpus rows.
All inputs are finite; a program needn't handle non-finite values.
Results may differ from the reference program's by a relative error of at most 0.007.
The reference program's roundings to bfloat16 on the way count: a program that leaves them out, or rounds other values in their place, can miss the bound.
Values may be sent and summed in bfloat16 or wider, within the bound.
No kernel may reach another device: no remote copies, remote signals or barrier semaphores. Data moves between devices by JAX's collectives and lax.ppermute only.
A program may use at most 128 MiB of HBM per device.

```python
import math
import jax
import jax.numpy as jnp
import numpy as np
from jax import lax

DIN = 28672
DOUT = 8192
RANK = 128
LONGEST = 64
K = 16384
P_SIZE = 128
TOK = 4096
R = 8192


def draw_corpus(key, part):
    first = jax.random.fold_in(jax.random.fold_in(key, 11), 0)
    base = jnp.clip(jax.random.normal(first, (R, K), jnp.float32), -6.0, 6.0)
    return base.astype(jnp.bfloat16)


def draw_owner(key, part):
    labels = jax.random.randint(jax.random.fold_in(key, 23), (R,), 0, 2 * P_SIZE).astype(jnp.int32)
    labels = labels.at[0].set(2 * P_SIZE - 1)
    labels = labels.at[R - 1].set(0)
    return labels


def level_of(rng, shape, shards, least, top_value):
    loudness, own = 1.0, jax.random.fold_in(rng, 6)
    for position, blocks in shards:
        draws = jnp.exp(jax.random.uniform(jax.random.fold_in(own, position), (blocks,), jnp.float32, least / len(shards), top_value / len(shards)))
        loudness = loudness * jnp.repeat(draws, shape[position] // blocks).reshape([-1 if axis == position else 1 for axis in range(len(shape))])
    return loudness


def length_profile(count, total, most, slope):
    portions = [(1 << 20) // math.isqrt(grade ** slope) + 1 for grade in range(2, count + 1)]
    rest, counts = total - most - (count - 1), [1] * (count - 1)
    while rest > 0:
        candidates = [i for i in range(count - 1) if counts[i] < most]
        mass, budget = sum([portions[i] for i in candidates]), rest
        for i in candidates:
            extra = min(most - counts[i], max(1, budget * portions[i] // mass), rest)
            counts[i] = counts[i] + extra
            rest = rest - extra
    return np.array([most] + counts)


def ragged(stream_key, amount, total, reach, slope):
    if amount == 2:
        one = jax.random.randint(stream_key, (), max(1, total - reach), min(reach, total - 1) + 1)
        return jnp.stack([one, total - one])
    sizes = jnp.asarray(length_profile(amount, total, reach, slope), jnp.int32)
    couples = (amount - 1) // 2
    source_of, receiver = sizes[1:1 + 2 * couples:2], sizes[2:2 + 2 * couples:2]
    slack = jnp.minimum(source_of - 1, reach - receiver)
    passed = jax.random.randint(jax.random.fold_in(stream_key, 1), (couples,), 0, 1 << 20) % (slack + 1)
    sizes = sizes.at[1:1 + 2 * couples:2].set(source_of - passed).at[2:2 + 2 * couples:2].set(receiver + passed)
    return sizes[jax.random.permutation(jax.random.fold_in(stream_key, 2), amount)]


def noise(key, extent, deviation, most, pieces=(), kind=jnp.bfloat16):
    factor_of = level_of(key, extent, pieces, -0.22, 0.18) if pieces else 1.0
    entries = jax.random.normal(key, extent, jnp.float32) * deviation * factor_of
    return jnp.minimum(jnp.maximum(entries, -most), most).astype(kind)


def setup_inputs(seed: int = 0, part: int = 0) -> dict:
    seeds = jax.random.split(jax.random.key(seed), 8)
    part_keys = jax.random.split(jax.random.fold_in(seeds[7], part), 8)
    return {
        "activations": noise(part_keys[0], (TOK, DIN), 1.0, 6.0, ((0, 4), (1, 4))),
        "out_grads": noise(part_keys[1], (TOK, DOUT), 1.0, 6.0, ((0, 4), (1, 4))),
        "proj_in": noise(part_keys[2], (DIN, RANK), DIN ** -0.5, 0.03125, ((0, 4),)),
        "proj_out": noise(part_keys[3], (DOUT, RANK), DOUT ** -0.5, 0.0625, ((0, 4),)),
        "lengths": ragged(part_keys[4], P_SIZE, TOK, LONGEST, 0).astype(jnp.int32),
        "corpus": draw_corpus(jax.random.fold_in(jax.random.fold_in(seeds[7], part), 71), part),
        "owner": draw_owner(jax.random.fold_in(seeds[7], 71), part),
    }


def reference(activations, out_grads, proj_in, proj_out, lengths, corpus, owner):
    x_low = jnp.dot(activations, proj_in, preferred_element_type=jnp.float32).astype(jnp.bfloat16)
    g_low = jnp.dot(out_grads, proj_out, preferred_element_type=jnp.float32).astype(jnp.bfloat16)
    ends = jnp.cumsum(lengths).astype(jnp.int32)
    starts = (ends - lengths).astype(jnp.int32)
    positions = jnp.arange(TOK, dtype=jnp.int32)
    member = ((positions[None, :] >= starts[:, None]) & (positions[None, :] < ends[:, None])).astype(jnp.bfloat16)

    def one_column(column):
        return jnp.dot(member * column[None, :], x_low, preferred_element_type=jnp.float32)
    stacked = lax.map(one_column, jnp.transpose(g_low))
    pgrad = jnp.transpose(stacked, (1, 0, 2)).reshape(P_SIZE, K)
    sumsq = lax.optimization_barrier(jnp.sum(pgrad * pgrad, axis=1))
    scale = 2.5 / math.sqrt(K) * lax.rsqrt(sumsq / K + 1e-06)
    raw = lax.dot_general(pgrad.astype(jnp.bfloat16), corpus, (((1,), (1,)), ((), ())), preferred_element_type=jnp.float32)
    score = raw * scale[:, None]
    owned = owner[None, :] == jnp.arange(P_SIZE, dtype=jnp.int32)[:, None]
    top = lax.optimization_barrier(jnp.max(jnp.where(owned, jnp.float32(-1e+30), score), axis=1))
    weight = jnp.where(owned, jnp.float32(0.0), jnp.exp(score - top[:, None]))
    total = lax.optimization_barrier(jnp.sum(weight, axis=1))
    summed = jnp.dot(weight.astype(jnp.bfloat16), corpus, preferred_element_type=jnp.float32)
    return summed / total[:, None]
```

```python
import functools
import math

import jax
import jax.numpy as jnp
from jax import lax
from jax.experimental import pallas as pl
from jax.experimental.pallas import tpu as pltpu
from jax.sharding import PartitionSpec as P

K = 16384
LONGEST = 64
LANES = 128
LOW = -1e30
F32, BF16 = jnp.float32, jnp.bfloat16
VMEM_BYTES = 48 * 1024 * 1024


def params():
    return pltpu.CompilerParams(vmem_limit_bytes=VMEM_BYTES)


def whole(shape):
    return pl.BlockSpec(shape, lambda *_: (0,) * len(shape))


def x_body(nfeat, per, me_ref, act_ref, proj_ref, *outs):
    i = pl.program_id(0)
    rows = act_ref.shape[0]
    part = jnp.dot(act_ref[...], proj_ref[...], preferred_element_type=F32)
    for j in range(nfeat):

        @pl.when(i // per == j)
        def _():
            outs[j][pl.ds(pl.multiple_of((i % per) * rows, rows), rows), :] = part


def project_x(me, act, proj, nfeat):
    tok, depth = act.shape
    rank = proj.shape[1]
    quarter = tok // nfeat
    rows = 128
    per = quarter // rows
    return pl.pallas_call(
        functools.partial(x_body, nfeat, per),
        grid_spec=pltpu.PrefetchScalarGridSpec(
            num_scalar_prefetch=1,
            grid=(tok // rows,),
            in_specs=[
                pl.BlockSpec((rows, depth), lambda i, me: (((me[0] + i // per) % nfeat) * per + i % per, 0)),
                whole((depth, rank)),
            ],
            out_specs=[whole((quarter, rank))] * nfeat,
        ),
        out_shape=[jax.ShapeDtypeStruct((quarter, rank), F32)] * nfeat,
        compiler_params=params(),
        cost_estimate=pl.CostEstimate(flops=2 * tok * depth * rank, bytes_accessed=2 * depth * (tok + rank), transcendentals=0),
        name="project_x",
    )(me, act, proj)


def g_body(nfeat, me_ref, grad_ref, proj_ref, *rest):
    outs, turned = rest[:nfeat], rest[nfeat]
    i = pl.program_id(0)
    rows = grad_ref.shape[0]
    width = outs[0].shape[0]
    part = jnp.dot(grad_ref[...], proj_ref[...], preferred_element_type=F32)
    turned[...] = jnp.transpose(part)
    for j in range(nfeat):
        f = lax.rem(me_ref[0] + j, nfeat)
        outs[j][:, pl.ds(pl.multiple_of(i * rows, rows), rows)] = turned[pl.ds(pl.multiple_of(f * width, width), width), :]


def project_g(me, grads, proj, nfeat):
    tok, depth = grads.shape
    rank = proj.shape[1]
    width = rank // nfeat
    rows = 256
    return pl.pallas_call(
        functools.partial(g_body, nfeat),
        grid_spec=pltpu.PrefetchScalarGridSpec(
            num_scalar_prefetch=1,
            grid=(tok // rows,),
            in_specs=[pl.BlockSpec((rows, depth), lambda i, me: (i, 0)), whole((depth, rank))],
            out_specs=[whole((width, tok))] * nfeat,
            scratch_shapes=[pltpu.VMEM((rank, rows), F32)],
        ),
        out_shape=[jax.ShapeDtypeStruct((width, tok), F32)] * nfeat,
        compiler_params=params(),
        cost_estimate=pl.CostEstimate(flops=2 * tok * depth * rank, bytes_accessed=2 * depth * (tok + rank), transcendentals=0),
        name="project_g",
    )(me, grads, proj)


def pgrad_body(nblk, passages, blk_ref, starts_ref, ends_ref, *rest):
    gs, xs = rest[:nblk], rest[nblk:2 * nblk]
    low_ref, sumsq_ref, g_all, x_all, grad = rest[2 * nblk:]
    width, tok = gs[0].shape
    total = nblk * tok
    for n in range(nblk):
        at = pl.multiple_of(blk_ref[n] * tok, tok)
        g_all[:, pl.ds(at, tok)] = gs[n][...]
        x_all[pl.ds(at, tok), :] = xs[n][...]
    group = LANES // width
    window = -(-group * LONGEST // LANES) * LANES + LANES

    def step(i, carry):
        first = i * group
        base = jnp.minimum((starts_ref[first] // LANES) * LANES, total - window)
        base = pl.multiple_of(base, LANES)
        g_part = g_all[:, pl.ds(base, window)].astype(F32)
        x_part = x_all[pl.ds(base, window), :]
        at = base + lax.broadcasted_iota(jnp.int32, (width, window), 1)
        stack = [
            jnp.where((at >= starts_ref[first + q]) & (at < ends_ref[first + q]), g_part, 0.0).astype(BF16)
            for q in range(group)
        ]
        grad[pl.ds(pl.multiple_of(i * LANES, LANES), LANES), :] = jnp.dot(
            jnp.concatenate(stack, axis=0), x_part, preferred_element_type=F32
        )
        return carry

    lax.fori_loop(0, passages // group, step, 0, unroll=4)
    squares = jnp.zeros((passages, LANES), F32)
    for a in range(width):
        column = grad[pl.ds(a, passages, stride=width), :]
        squares = squares + column * column
        low_ref[:, a * LANES:(a + 1) * LANES] = column.astype(BF16)
    sums = jnp.sum(jnp.transpose(squares), axis=0, keepdims=True)
    sumsq_ref[...] = jnp.broadcast_to(sums, sumsq_ref.shape)


def passage_grads(blocks, starts, ends, gs, xs):
    nblk = len(gs)
    width, tok = gs[0].shape
    rank = xs[0].shape[1]
    passages = starts.shape[0]
    return pl.pallas_call(
        functools.partial(pgrad_body, nblk, passages),
        grid_spec=pltpu.PrefetchScalarGridSpec(
            num_scalar_prefetch=3,
            grid=(),
            in_specs=[pl.BlockSpec(memory_space=pltpu.VMEM)] * (2 * nblk),
            out_specs=[pl.BlockSpec(memory_space=pltpu.VMEM)] * 2,
            scratch_shapes=[
                pltpu.VMEM((width, nblk * tok), BF16),
                pltpu.VMEM((nblk * tok, rank), BF16),
                pltpu.VMEM((passages * width, rank), F32),
            ],
        ),
        out_shape=[
            jax.ShapeDtypeStruct((passages, width * rank), BF16),
            jax.ShapeDtypeStruct((8, passages), F32),
        ],
        compiler_params=params(),
        cost_estimate=pl.CostEstimate(flops=8 * passages * width * LONGEST * 6 * rank, bytes_accessed=2 * nblk * tok * (rank + width), transcendentals=0),
        name="passage_grads",
    )(blocks, starts, ends, *gs, *xs)


def score_body(me_ref, grad_ref, corpus_ref, out_ref):
    out_ref[...] = lax.dot_general(
        grad_ref[...], corpus_ref[...], (((1,), (1,)), ((), ())), preferred_element_type=F32
    )


def score_part(me, low, corpus, j, nfeat):
    passages, depth = low.shape
    quarter = corpus.shape[0] // nfeat
    rows = 256
    per = quarter // rows
    return pl.pallas_call(
        score_body,
        grid_spec=pltpu.PrefetchScalarGridSpec(
            num_scalar_prefetch=1,
            grid=(per,),
            in_specs=[
                whole((passages, depth)),
                pl.BlockSpec((rows, depth), lambda i, me: (((me[0] + j) % nfeat) * per + i, 0)),
            ],
            out_specs=pl.BlockSpec((passages, rows), lambda i, me: (0, i)),
        ),
        out_shape=jax.ShapeDtypeStruct((passages, quarter), F32),
        compiler_params=params(),
        cost_estimate=pl.CostEstimate(flops=2 * passages * depth * quarter, bytes_accessed=2 * depth * quarter, transcendentals=0),
        name="score_part",
    )(me, low, corpus)


def split3(value):
    high = value.astype(BF16)
    rest = value - high.astype(F32)
    middle = rest.astype(BF16)
    return high, middle, (rest - middle.astype(F32)).astype(BF16)


def pack_stats(top, total):
    lane = lax.broadcasted_iota(jnp.int32, (top.shape[0], LANES), 1)
    tile = jnp.zeros((top.shape[0], LANES), F32)
    for n, piece in enumerate(split3(top) + split3(total)):
        tile = jnp.where(lane == n, piece.astype(F32), tile)
    return tile.astype(BF16)


def unpack_stats(tile):
    tile = tile.astype(F32)
    top = (tile[:, 0:1] + tile[:, 1:2]) + tile[:, 2:3]
    total = (tile[:, 3:4] + tile[:, 4:5]) + tile[:, 5:6]
    return top, total


def weight_body(nfeat, owner_ref, *rest):
    parts, squares, out_ref = rest[:nfeat], rest[nfeat:2 * nfeat], rest[2 * nfeat]
    passages, rows = parts[0].shape
    raw = parts[0][...]
    sumsq = squares[0][0:1, :]
    for n in range(1, nfeat):
        raw = raw + parts[n][...]
        sumsq = sumsq + squares[n][0:1, :]
    scale = 2.5 / math.sqrt(K) * lax.rsqrt(sumsq / K + 1e-06)
    scale = jnp.transpose(jnp.broadcast_to(scale, (LANES, passages)))[:, 0:1]
    owned = owner_ref[...] == lax.broadcasted_iota(jnp.int32, (passages, rows), 0)
    score = jnp.where(owned, LOW, raw * scale)
    top = jnp.max(score, axis=1, keepdims=True)
    weight = jnp.where(owned, 0.0, jnp.exp(score - top))
    total = jnp.sum(weight, axis=1, keepdims=True)
    out_ref[:, :rows] = weight.astype(BF16)
    out_ref[:, rows:] = pack_stats(top, total)


def weights_of(owner, parts, squares):
    passages, rows = parts[0].shape
    return pl.pallas_call(
        functools.partial(weight_body, len(parts)),
        in_specs=[pl.BlockSpec(memory_space=pltpu.VMEM)] * (1 + 2 * len(parts)),
        out_specs=pl.BlockSpec(memory_space=pltpu.VMEM),
        out_shape=jax.ShapeDtypeStruct((passages, rows + LANES), BF16),
        compiler_params=params(),
        cost_estimate=pl.CostEstimate(flops=8 * passages * rows, bytes_accessed=16 * passages * rows, transcendentals=passages * rows),
        name="weights",
    )(owner, *parts, *squares)


def influence_body(nfeat, nrows, nsub, place_ref, *rest):
    pieces, corpus_ref, send_ref, keep_ref, total_sum = rest[:nfeat], *rest[nfeat:]
    i = pl.program_id(0)
    passages = pieces[0].shape[0]
    quarter = pieces[0].shape[1] - LANES
    cols = corpus_ref.shape[1]
    span = send_ref.shape[1]
    depth = send_ref.shape[2] - LANES
    me, core = place_ref[0], place_ref[1]
    stats = [unpack_stats(p[:, quarter:]) for p in pieces]
    top = functools.reduce(jnp.maximum, [s[0] for s in stats])
    factors = [jnp.exp(s[0] - top) for s in stats]
    total = sum(f * s[1] for f, s in zip(factors, stats))
    share = 1.0 / jnp.maximum(total, 1e-30)
    acc = jnp.zeros((passages, cols), F32)
    for j in range(nfeat):
        source = lax.rem(me + nfeat - j, nfeat)
        rows = corpus_ref[pl.ds(pl.multiple_of(source * quarter, quarter), quarter), :]
        acc = acc + (factors[j] * share) * jnp.dot(pieces[j][:, :quarter], rows, preferred_element_type=F32)
    total_sum[...] = acc
    at = pl.ds(pl.multiple_of(i * cols, cols), cols)
    for x in range(nrows):
        mine = pl.multiple_of((x * nsub + core) * span, span)
        other = pl.multiple_of((x * nsub + (nsub - 1 - core)) * span, span)
        keep_ref[x, :, at] = total_sum[pl.ds(mine, span), :]
        send_ref[x, :, at] = total_sum[pl.ds(other, span), :].astype(BF16)

    @pl.when(i == 0)
    def _():
        lane = lax.broadcasted_iota(jnp.int32, (passages, LANES), 1)
        total_sum[:, 0:LANES] = jnp.where(lane == 0, top, total)
        for x in range(nrows):
            mine = pl.multiple_of((x * nsub + core) * span, span)
            other = pl.multiple_of((x * nsub + (nsub - 1 - core)) * span, span)
            keep_ref[x, :, depth:] = total_sum[pl.ds(mine, span), 0:LANES]
            tile = total_sum[pl.ds(other, span), 0:LANES]
            send_ref[x, :, depth:] = pack_stats(tile[:, 0:1], tile[:, 1:2])


def influence_parts(place, pieces, corpus, nrows, nsub):
    passages = pieces[0].shape[0]
    rows, depth = corpus.shape
    span = passages // (nrows * nsub)
    cols = 512
    shape = (nrows, span, depth + LANES)
    return pl.pallas_call(
        functools.partial(influence_body, len(pieces), nrows, nsub),
        grid_spec=pltpu.PrefetchScalarGridSpec(
            num_scalar_prefetch=1,
            grid=(depth // cols,),
            in_specs=[whole(p.shape) for p in pieces] + [pl.BlockSpec((rows, cols), lambda i, place: (0, i))],
            out_specs=[whole(shape)] * 2,
            scratch_shapes=[pltpu.VMEM((passages, cols), F32)],
        ),
        out_shape=[jax.ShapeDtypeStruct(shape, BF16), jax.ShapeDtypeStruct(shape, F32)],
        compiler_params=params(),
        cost_estimate=pl.CostEstimate(flops=2 * passages * rows * depth, bytes_accessed=2 * rows * depth, transcendentals=0),
        name="influence_parts",
    )(place, *pieces, corpus)


def merge_two(keep, other):
    depth = keep.shape[1] - LANES
    top_a, total_a = keep[:, depth:depth + 1], keep[:, depth + 1:depth + 2]
    top_b, total_b = unpack_stats(other[:, depth:])
    top = jnp.maximum(top_a, top_b)
    part_a, part_b = total_a * jnp.exp(top_a - top), total_b * jnp.exp(top_b - top)
    total = part_a + part_b
    share = 1.0 / jnp.maximum(total, 1e-30)
    value = keep[:, :depth] * (part_a * share) + other[:, :depth].astype(F32) * (part_b * share)
    return value, top, total


def merge_core_body(place_ref, keep_ref, other_ref, send_ref, next_ref):
    depth = send_ref.shape[1] - LANES
    mine = place_ref[2]
    value, top, total = merge_two(keep_ref[1 - mine], other_ref[1 - mine])
    send_ref[:, :depth] = value.astype(BF16)
    send_ref[:, depth:] = pack_stats(top, total)
    value, top, total = merge_two(keep_ref[mine], other_ref[mine])
    lane = lax.broadcasted_iota(jnp.int32, (value.shape[0], LANES), 1)
    next_ref[:, :depth] = value
    next_ref[:, depth:] = jnp.where(lane == 0, top, total)


def merge_core(place, keep, other):
    shape = keep.shape[1:]
    return pl.pallas_call(
        merge_core_body,
        grid_spec=pltpu.PrefetchScalarGridSpec(
            num_scalar_prefetch=1,
            grid=(),
            in_specs=[pl.BlockSpec(memory_space=pltpu.VMEM)] * 2,
            out_specs=[pl.BlockSpec(memory_space=pltpu.VMEM)] * 2,
        ),
        out_shape=[jax.ShapeDtypeStruct(shape, BF16), jax.ShapeDtypeStruct(shape, F32)],
        compiler_params=params(),
        name="merge_core",
    )(place, keep, other)


def merge_last_body(keep_ref, other_ref, out_ref):
    out_ref[...] = merge_two(keep_ref[...], other_ref[...])[0]


def merge_last(keep, other):
    return pl.pallas_call(
        merge_last_body,
        in_specs=[pl.BlockSpec(memory_space=pltpu.VMEM)] * 2,
        out_specs=pl.BlockSpec(memory_space=pltpu.VMEM),
        out_shape=jax.ShapeDtypeStruct((keep.shape[0], keep.shape[1] - LANES), F32),
        compiler_params=params(),
        name="merge_last",
    )(keep, other)


def shift(value, axis, by):
    count = lax.axis_size(axis)
    return lax.ppermute(value, axis, [(i, (i + by) % count) for i in range(count)])


def scatter_parts(blocks):
    return [blocks[0]] + [shift(blocks[j], "feat", j) for j in range(1, len(blocks))]


def gather_parts(piece, nfeat):
    return [piece] + [shift(piece, "feat", j) for j in range(1, nfeat)]


def gather_blocks(piece, nrows, nsub):
    across = [piece] + [shift(piece, "rows", d) for d in range(1, nrows)]
    beside = [shift(p, "sub", 1) for p in across]
    return across + beside, [(d, 0) for d in range(nrows)] + [(d, 1) for d in range(nrows)]


def fast(activations, out_grads, proj_in, proj_out, lengths, corpus, owner):
    nfeat, nrows, nsub = (lax.axis_size(a) for a in ("feat", "rows", "sub"))
    feat, row, sub = (lax.axis_index(a).astype(jnp.int32) for a in ("feat", "rows", "sub"))
    me = feat.reshape(1)
    place = jnp.stack([feat, sub, row])
    ends = jnp.cumsum(lengths)
    starts = ends - lengths
    quarter = corpus.shape[0] // nfeat
    owner_here = lax.dynamic_slice_in_dim(owner, feat * quarter, quarter, 0).reshape(1, quarter)

    g_parts = scatter_parts(project_g(me, out_grads, proj_out, nfeat))
    x_parts = scatter_parts(project_x(me, activations, proj_in, nfeat))
    g_low = functools.reduce(jnp.add, g_parts).astype(BF16)
    g_blocks, back = gather_blocks(g_low, nrows, nsub)
    x_piece = functools.reduce(jnp.add, x_parts).astype(BF16)
    pieces = gather_parts(x_piece, nfeat)
    per = x_piece.shape[0]
    x_low = jnp.zeros((per * nfeat, x_piece.shape[1]), BF16)
    for j, piece in enumerate(pieces):
        x_low = lax.dynamic_update_slice_in_dim(x_low, piece, lax.rem(feat + nfeat - j, nfeat) * per, 0)
    x_blocks, _ = gather_blocks(x_low, nrows, nsub)
    blocks = jnp.stack([lax.rem(row + nrows - d, nrows) * nsub + lax.rem(sub + nsub - c, nsub) for d, c in back])
    low, sumsq = passage_grads(blocks, starts, ends, g_blocks, x_blocks)
    squares = gather_parts(sumsq, nfeat)
    raw = [None] * nfeat
    for j in list(range(1, nfeat)) + [0]:
        raw[j] = score_part(me, low, corpus, j, nfeat)
    weight = weights_of(owner_here, scatter_parts(raw), squares)
    send, keep = influence_parts(place, gather_parts(weight, nfeat), corpus, nrows, nsub)
    send, keep = merge_core(place, keep, shift(send, "sub", 1))
    return merge_last(keep, shift(send, "rows", 1))


def general(activations, out_grads, proj_in, proj_out, lengths, corpus, owner):
    tok_local = activations.shape[0]
    passages = lengths.shape[0]
    nfeat = lax.axis_size("feat")
    part_x = jnp.dot(activations, proj_in, preferred_element_type=F32)
    part_g = jnp.dot(out_grads, proj_out, preferred_element_type=F32)
    width_cols = part_g.shape[1] // nfeat
    x_low = lax.psum(part_x, "feat").astype(BF16)
    g_low = lax.psum_scatter(part_g, "feat", scatter_dimension=1, tiled=True).astype(BF16)
    ends = jnp.cumsum(lengths)
    starts = ends - lengths
    positions = lax.axis_index(("rows", "sub")) * tok_local + jnp.arange(tok_local, dtype=jnp.int32)
    member = ((positions[None, :] >= starts[:, None]) & (positions[None, :] < ends[:, None])).astype(BF16)
    scaled_member = member[None, :, :] * jnp.transpose(g_low)[:, None, :]
    partial_grad = jnp.einsum("apt,tb->pab", scaled_member, x_low, preferred_element_type=F32)
    partial_grad = partial_grad.reshape(passages, width_cols * x_low.shape[1])
    pgrad = lax.psum(partial_grad, ("rows", "sub"))
    pgrad_low = pgrad.astype(BF16)
    sumsq_part = jnp.sum(pgrad * pgrad, axis=1)
    raw_part = lax.dot_general(pgrad_low, corpus, (((1,), (1,)), ((), ())), preferred_element_type=F32)
    labels = jnp.arange(passages, dtype=jnp.int32)[:, None]
    raw, sumsq = lax.psum((raw_part, sumsq_part), "feat")
    scale = 2.5 / math.sqrt(K) * lax.rsqrt(sumsq / K + 1e-06)
    score = raw * scale[:, None]
    owned = owner[None, :] == labels
    top = lax.pmax(jnp.max(jnp.where(owned, F32(LOW), score), axis=1), ("rows", "sub"))
    weight = jnp.where(owned, F32(0.0), jnp.exp(score - top[:, None]))
    total = lax.psum(jnp.sum(weight, axis=1), ("rows", "sub"))
    span = passages // lax.axis_size(("rows", "sub"))
    summed = lax.psum_scatter(
        jnp.dot(weight.astype(BF16), corpus, preferred_element_type=F32),
        ("rows", "sub"),
        scatter_dimension=0,
        tiled=True,
    )
    own_total = lax.dynamic_slice_in_dim(total, lax.axis_index(("rows", "sub")) * span, span, 0)
    return summed / own_total[:, None]


def solution(mesh):
    small = mesh.shape["feat"] <= 4 and mesh.shape["rows"] == 2 and mesh.shape["sub"] == 2
    return jax.shard_map(
        fast if small else general,
        mesh=mesh,
        in_specs=(
            P(("groups", "rows", "sub"), "feat"),
            P(("groups", "rows", "sub"), "feat"),
            P(("groups", "feat"), None),
            P(("groups", "feat"), None),
            P("groups"),
            P(("groups", "rows", "sub"), "feat"),
            P(("rows", "sub")),
        ),
        out_specs=P(("groups", "rows", "sub"), "feat"),
        check_vma=False,
    )
```

```python
import functools
import math

import jax
import jax.numpy as jnp
from jax import lax
from jax.experimental import pallas as pl
from jax.experimental.pallas import tpu as pltpu
from jax.sharding import PartitionSpec as P

K = 16384
LONGEST = 64
LANES = 128
LOW = -1e30
F32, BF16 = jnp.float32, jnp.bfloat16
MIB = 1024 * 1024
CODES = 16
STEP = 369.0
FULL = 32767.0


def params(mib=16):
    return pltpu.CompilerParams(vmem_limit_bytes=mib * MIB)


def whole(shape):
    return pl.BlockSpec(shape, lambda *_: (0,) * len(shape))


VMEM = pl.BlockSpec(memory_space=pltpu.VMEM)
ANY = pl.BlockSpec(memory_space=pl.ANY)
HBM = pl.BlockSpec(memory_space=pltpu.HBM)


def level_of(value):
    return jnp.floor(jnp.log(jnp.maximum(value, 1e-30)) * STEP)


def value_of(level):
    return jnp.exp(level * (1.0 / STEP))


def to_short(value):
    return jnp.floor(value + 0.5).astype(jnp.int32).astype(jnp.int16)


def from_short(value):
    return value.astype(jnp.int32).astype(F32)


def scale_level(peak):
    return level_of(peak) + 2.0


def turned_dot(proj_t, tokens):
    return lax.dot_general(proj_t, tokens, (((1,), (1,)), ((), ())), preferred_element_type=F32)


def rows_of(total, count):
    return [pl.ds(n * (total // count), total // count) for n in range(count)]


def eye(size):
    return jnp.where(
        lax.broadcasted_iota(jnp.int32, (size, size), 0) == lax.broadcasted_iota(jnp.int32, (size, size), 1), 1.0, 0.0
    ).astype(BF16)


def turn_low(value):
    return turned_dot(eye(value.shape[1]), value).astype(BF16)


def x_body(nfeat, steps, ahead, me_ref, act_hbm, proj_hbm, own_ref, *rest):
    outs, (acts, proj, total, act_sems, proj_sems) = rest[:nfeat - 1], rest[nfeat - 1:]
    rank, quarter = own_ref.shape
    depth = proj_hbm.shape[0]
    chunks = rows_of(depth, steps)
    loads = [pltpu.make_async_copy(act_hbm.at[:, c], acts.at[n], act_sems.at[n]) for n, c in enumerate(chunks)]
    proj_loads = [pltpu.make_async_copy(proj_hbm.at[c, :], proj.at[n], proj_sems.at[n]) for n, c in enumerate(chunks)]
    for n in range(ahead):
        proj_loads[n].start()
        loads[n].start()
    for n in range(steps):
        proj_loads[n].wait()
        proj_t = turn_low(proj[n])
        loads[n].wait()
        if n + ahead < steps:
            proj_loads[n + ahead].start()
            loads[n + ahead].start()
        part = turned_dot(proj_t, acts[n])
        total[...] = part if n == 0 else total[...] + part
    for j in range(nfeat):
        to = lax.rem(me_ref[0] + j, nfeat)
        value = total[:, pl.ds(pl.multiple_of(to * quarter, quarter), quarter)]
        if j == 0:
            own_ref[...] = value
        else:
            level = scale_level(jnp.max(jnp.abs(value), axis=0, keepdims=True))
            outs[j - 1][:rank, :] = to_short(value * (FULL / value_of(level)))
            outs[j - 1][rank:, :] = jnp.broadcast_to(level, (CODES, quarter)).astype(jnp.int32).astype(jnp.int16)


def project_x(me, act, proj, nfeat):
    tok, depth = act.shape
    rank = proj.shape[1]
    quarter = tok // nfeat
    steps = 7
    chunk = depth // steps
    return pl.pallas_call(
        functools.partial(x_body, nfeat, steps, 3),
        grid_spec=pltpu.PrefetchScalarGridSpec(
            num_scalar_prefetch=1,
            grid=(),
            in_specs=[HBM, HBM],
            out_specs=[VMEM] * nfeat,
            scratch_shapes=[
                pltpu.VMEM((steps, tok, chunk), BF16),
                pltpu.VMEM((steps, chunk, rank), BF16),
                pltpu.VMEM((rank, tok), F32),
                pltpu.SemaphoreType.DMA((steps,)),
                pltpu.SemaphoreType.DMA((steps,)),
            ],
        ),
        out_shape=[jax.ShapeDtypeStruct((rank, quarter), F32)]
        + [jax.ShapeDtypeStruct((rank + CODES, quarter), jnp.int16)] * (nfeat - 1),
        compiler_params=params(52),
        cost_estimate=pl.CostEstimate(flops=2 * tok * depth * rank, bytes_accessed=2 * depth * (tok + rank), transcendentals=0),
        name="project_x",
    )(me, act, proj)


def g_body(nfeat, steps, me_ref, grad_hbm, proj_hbm, starts_ref, ends_ref, own_ref, *rest):
    outs, (grads, proj, turned, grad_sems, proj_sem) = rest[:nfeat - 1], rest[nfeat - 1:]
    width, tok = own_ref.shape
    rows = rows_of(tok, steps)
    proj_load = pltpu.make_async_copy(proj_hbm, proj, proj_sem)
    proj_load.start()
    loads = [pltpu.make_async_copy(grad_hbm.at[r, :], grads.at[r, :], grad_sems.at[n]) for n, r in enumerate(rows)]
    for load in loads:
        load.start()
    proj_load.wait()
    proj_t = turn_low(proj[...])
    for n in range(0, steps, 2):
        loads[n].wait()
        loads[n + 1].wait()
        at = slice(n * tok // steps, (n + 2) * tok // steps)
        turned[:, at] = turned_dot(proj_t, grads[at, :])
    chunks = tok // LANES
    for j in range(nfeat):
        to = lax.rem(me_ref[0] + j, nfeat)
        at = pl.ds(pl.multiple_of(to * width, width), width)
        if j == 0:
            own_ref[...] = turned[at, :]
        else:
            parts = [turned[at, n * LANES:(n + 1) * LANES] for n in range(chunks)]
            peak = functools.reduce(jnp.maximum, [jnp.abs(p) for p in parts])
            level = scale_level(jnp.max(peak, axis=0, keepdims=True))
            factor = FULL / value_of(level)
            for n in range(chunks):
                outs[j - 1][n * width:(n + 1) * width, :] = to_short(parts[n] * factor)
            outs[j - 1][chunks * width:, :] = jnp.broadcast_to(level, (CODES, LANES)).astype(jnp.int32).astype(jnp.int16)


def project_g(me, grads, proj, nfeat, *after):
    tok, depth = grads.shape
    rank = proj.shape[1]
    width = rank // nfeat
    steps = 4
    short = (tok // LANES * width + CODES, LANES)
    return pl.pallas_call(
        functools.partial(g_body, nfeat, steps),
        grid_spec=pltpu.PrefetchScalarGridSpec(
            num_scalar_prefetch=1,
            grid=(),
            in_specs=[HBM, HBM] + [ANY] * len(after),
            out_specs=[VMEM] * nfeat,
            scratch_shapes=[
                pltpu.VMEM((tok, depth), BF16),
                pltpu.VMEM((depth, rank), BF16),
                pltpu.VMEM((rank, tok), F32),
                pltpu.SemaphoreType.DMA((steps,)),
                pltpu.SemaphoreType.DMA,
            ],
        ),
        out_shape=[jax.ShapeDtypeStruct((width, tok), F32)] + [jax.ShapeDtypeStruct(short, jnp.int16)] * (nfeat - 1),
        compiler_params=params(53),
        cost_estimate=pl.CostEstimate(flops=2 * tok * depth * rank, bytes_accessed=2 * depth * (tok + rank), transcendentals=0),
        name="project_g",
    )(me, grads, proj, *after)


def join_x_body(nafter, *refs):
    own_ref, others, out_ref = refs[nafter], refs[nafter + 1:-1], refs[-1]
    rows = own_ref.shape[0]
    value = own_ref[...]
    for other in others:
        scale = value_of(from_short(other[rows:, :])[0:1, :]) * (1.0 / FULL)
        value = value + from_short(other[:rows, :]) * scale
    out_ref[...] = value.astype(BF16)


def join_g_body(nafter, *refs):
    own_ref, others, out_ref = refs[nafter], refs[nafter + 1:-1], refs[-1]
    width, tok = own_ref.shape
    chunks = tok // LANES
    scales = [value_of(from_short(other[chunks * width:, :])[0:1, :]) * (1.0 / FULL) for other in others]
    for c in range(chunks):
        value = own_ref[:, c * LANES:(c + 1) * LANES]
        for other, scale in zip(others, scales):
            value = value + from_short(other[c * width:(c + 1) * width, :]) * scale
        out_ref[:, c * LANES:(c + 1) * LANES] = value.astype(BF16)


def join(body, parts, after=()):
    return pl.pallas_call(
        functools.partial(body, len(after)),
        in_specs=[ANY] * len(after) + [VMEM] * len(parts),
        out_specs=VMEM,
        out_shape=jax.ShapeDtypeStruct(parts[0].shape, BF16),
        compiler_params=params(),
        name=body.__name__,
    )(*after, *parts)


def pack_body(x_refs, *rest):
    pieces, more, out_ref = rest[:x_refs], rest[x_refs:-1], rest[-1]
    size = pieces[0].shape[1]
    for n, piece in enumerate(pieces):
        out_ref[:, n * size:(n + 1) * size] = piece[...]
    for ref in more:
        rows = ref.shape[0]
        for n in range(ref.shape[1] // size):
            out_ref[n * rows:(n + 1) * rows, x_refs * size:] = ref[:, n * size:(n + 1) * size]


def pack(pieces, more=()):
    rows, size = pieces[0].shape
    count = len(pieces) + len(more)
    return pl.pallas_call(
        functools.partial(pack_body, len(pieces)),
        in_specs=[VMEM] * count,
        out_specs=VMEM,
        out_shape=jax.ShapeDtypeStruct((rows, count * size), BF16),
        compiler_params=params(),
        name="pack",
    )(*pieces, *more)


def token_body(width, me_ref, first_ref, last_ref, *rest):
    out_ref = rest[-1]
    rank = first_ref.shape[0]
    size = last_ref.shape[1] // 2
    pieces = [first_ref[:, n * size:(n + 1) * size] for n in range(3)] + [last_ref[:, :size]]
    for source, piece in zip(sources_of(me_ref[0]), pieces):
        out_ref[:rank, pl.ds(pl.multiple_of(source * size, size), size)] = piece
    for n in range(rank // width):
        out_ref[rank:, n * size:(n + 1) * size] = last_ref[n * width:(n + 1) * width, size:]


def token_block(me, first, last, width, after=()):
    rank, size = last.shape
    return pl.pallas_call(
        functools.partial(token_body, width),
        grid_spec=pltpu.PrefetchScalarGridSpec(
            num_scalar_prefetch=1, grid=(), in_specs=[VMEM] * 2 + [ANY] * len(after), out_specs=VMEM
        ),
        out_shape=jax.ShapeDtypeStruct((rank + width, rank // width * size // 2), BF16),
        compiler_params=params(),
        name="token_block",
    )(me, first, last, *after)


def turn(row):
    return jnp.transpose(jnp.broadcast_to(row, (LANES, row.shape[1])))[:, 0:1]


def turn_back(column):
    return jnp.transpose(jnp.broadcast_to(column, (column.shape[0], LANES)))[0:1, :]


def norm_of(sumsq):
    return sumsq / K + 1e-06


def spread(row, lanes):
    return jnp.concatenate([row] * (lanes // row.shape[1]), axis=1)


def code_rows(rows, lanes):
    at = lax.broadcasted_iota(jnp.int32, (CODES, lanes), 0)
    tile = jnp.zeros((CODES, lanes), F32)
    for n, row in enumerate(rows):
        tile = jnp.where(at == n, spread(row, lanes), tile)
    return tile


def loads_of(corpus_hbm, corpus_ref, sems, quarters, halves):
    size = corpus_ref.shape[1]
    loads = []
    for n, quarter in enumerate(quarters):
        rows = pl.ds(pl.multiple_of(quarter * size, size), size)
        for h, here in enumerate(rows_of(corpus_ref.shape[2], halves)):
            loads.append(pltpu.make_async_copy(corpus_hbm.at[rows, here], corpus_ref.at[n, :, here], sems.at[n * halves + h]))
    return loads


def write_scores(value, sumsq, out_ref):
    passages, quarter = value.shape
    coarse = level_of(sumsq)
    fine = jnp.floor((jnp.maximum(sumsq, 1e-30) / value_of(coarse) - 1.0) * (2.0**22))
    level = scale_level(jnp.max(jnp.abs(value), axis=0, keepdims=True))
    out_ref[:passages, :] = to_short(value * (FULL / value_of(level)))
    out_ref[passages:, :] = code_rows([level, coarse, fine], quarter).astype(jnp.int32).astype(jnp.int16)


def hold_body(me_ref, corpus_hbm, after_ref, held_ref, sem):
    size = held_ref.shape[0]
    load = pltpu.make_async_copy(corpus_hbm.at[pl.ds(pl.multiple_of(me_ref[0] * size, size), size), :], held_ref, sem)
    load.start()
    load.wait()


def hold(me, corpus, nfeat, after):
    rows, depth = corpus.shape
    return pl.pallas_call(
        hold_body,
        grid_spec=pltpu.PrefetchScalarGridSpec(
            num_scalar_prefetch=1,
            grid=(),
            in_specs=[HBM, ANY],
            out_specs=VMEM,
            scratch_shapes=[pltpu.SemaphoreType.DMA],
        ),
        out_shape=jax.ShapeDtypeStruct((rows // nfeat, depth), BF16),
        compiler_params=params(34),
        cost_estimate=pl.CostEstimate(flops=0, bytes_accessed=4 * rows // nfeat * depth, transcendentals=0),
        name="hold",
    )(me, corpus, after)


def first_body(nblk, passages, place_ref, starts_ref, ends_ref, *rest):
    blocks, corpus_hbm = rest[:nblk], rest[nblk]
    out_ref, sumsq_ref, low, held_ref, corpus_ref, tokens, grad, sems, held_sems = rest[nblk + 1:]
    me = place_ref[0]
    sources = sources_of(me)
    loads = loads_of(corpus_hbm, corpus_ref, sems, sources[3:], 1)
    later = loads_of(corpus_hbm, held_ref, held_sems, sources[1:3], 1)
    for load in loads + later:
        load.start()

    height, tok = blocks[0].shape
    rank = height - low.shape[1] // LANES
    width = height - rank
    for n in range(nblk):
        tokens[:, pl.ds(pl.multiple_of(place_ref[3 + n] * tok, tok), tok)] = blocks[n][...]
    group = LANES // width
    window = -(-group * LONGEST // LANES) * LANES + LANES

    def step(i, carry):
        first = i * group
        base = jnp.minimum((starts_ref[first] // LANES) * LANES, nblk * tok - window)
        here = pl.ds(pl.multiple_of(base, LANES), window)
        g_part = tokens[rank:, here]
        token = base + lax.broadcasted_iota(jnp.int32, (CODES, window), 1)
        stack = []
        for q in range(group):
            inside = (token >= starts_ref[first + q]) & (token < ends_ref[first + q])
            member = jnp.where(inside, 1.0, 0.0).astype(BF16)
            stack.append(g_part * jnp.concatenate([member] * (width // CODES), axis=0))
        grad[pl.ds(pl.multiple_of(i * LANES, LANES), LANES), :] = lax.dot_general(
            jnp.concatenate(stack, axis=0), tokens[:rank, here], (((1,), (1,)), ((), ())), preferred_element_type=F32
        )
        return carry

    lax.fori_loop(0, passages // group, step, 0, unroll=4)
    squares = jnp.zeros((passages, LANES), F32)
    for a in range(width):
        column = grad[pl.ds(a, passages, stride=width), :]
        squares = squares + column * column
        low[:, a * LANES:(a + 1) * LANES] = column.astype(BF16)
    sumsq = jnp.sum(jnp.transpose(squares), axis=0, keepdims=True)
    sumsq_ref[...] = jnp.broadcast_to(sumsq, sumsq_ref.shape)
    norm = turn(lax.rsqrt(norm_of(sumsq)))
    for load in loads:
        load.wait()
    write_scores(norm * turned_dot(low[...], corpus_ref[0]), sumsq, out_ref)
    for load in later:
        load.wait()


def first_scores(place, starts, ends, blocks, corpus, nfeat):
    passages = starts.shape[0]
    rows, depth = corpus.shape
    quarter = rows // nfeat
    height, tok = blocks[0].shape
    nblk = len(blocks)
    return pl.pallas_call(
        functools.partial(first_body, nblk, passages),
        grid_spec=pltpu.PrefetchScalarGridSpec(
            num_scalar_prefetch=3,
            grid=(),
            in_specs=[VMEM] * nblk + [HBM],
            out_specs=[VMEM] * 4,
            scratch_shapes=[
                pltpu.VMEM((1, quarter, depth), BF16),
                pltpu.VMEM((height, nblk * tok), BF16),
                pltpu.VMEM((passages * depth // LANES, LANES), F32),
                pltpu.SemaphoreType.DMA((1,)),
                pltpu.SemaphoreType.DMA((nfeat - 2,)),
            ],
        ),
        out_shape=[
            jax.ShapeDtypeStruct((passages + CODES, quarter), jnp.int16),
            jax.ShapeDtypeStruct((8, passages), F32),
            jax.ShapeDtypeStruct((passages, depth), BF16),
            jax.ShapeDtypeStruct((nfeat - 2, quarter, depth), BF16),
        ],
        compiler_params=params(30),
        cost_estimate=pl.CostEstimate(flops=2 * passages * depth * rows, bytes_accessed=rows * depth, transcendentals=0),
        name="first_scores",
    )(place, starts, ends, *blocks, corpus)


def near_body(low_ref, sumsq_ref, held_own_ref, held_ref, own_ref, across_ref, beside_ref):
    sumsq = sumsq_ref[0:1, :]
    norm = turn(lax.rsqrt(norm_of(sumsq)))
    write_scores(norm * turned_dot(low_ref[...], held_ref[0]), sumsq, beside_ref)
    across_ref[...] = norm * turned_dot(low_ref[...], held_ref[1])
    own_ref[...] = norm * turned_dot(low_ref[...], held_own_ref[...])


def near_scores(low, sumsq, held_own, held):
    passages, depth = low.shape
    quarter = held.shape[1]
    return pl.pallas_call(
        near_body,
        in_specs=[VMEM] * 4,
        out_specs=[VMEM] * 3,
        out_shape=[jax.ShapeDtypeStruct((passages, quarter), F32)] * 2
        + [jax.ShapeDtypeStruct((passages + CODES, quarter), jnp.int16)],
        compiler_params=params(8),
        cost_estimate=pl.CostEstimate(flops=6 * passages * depth * quarter, bytes_accessed=6 * quarter * depth, transcendentals=0),
        name="near_scores",
    )(low, sumsq, held_own, held)


def split3(value):
    high = value.astype(BF16)
    rest = value - high.astype(F32)
    middle = rest.astype(BF16)
    return [p.astype(F32) for p in (high, middle, (rest - middle.astype(F32)).astype(BF16))]


def pack_level(tile):
    lane = lax.broadcasted_iota(jnp.int32, tile.shape, 1)
    out = jnp.zeros(tile.shape, F32)
    for n, piece in enumerate(split3(tile)):
        out = jnp.where(lane == n, piece, out)
    return out.astype(BF16)


def unpack_level(tile):
    return jnp.broadcast_to(jnp.sum(tile.astype(F32), axis=1, keepdims=True), tile.shape)


def read_scores(ref):
    passages = ref.shape[0] - CODES
    code = from_short(ref[passages:, :])
    base = value_of(code[1:2, :passages])
    square = base + base * (code[2:3, :passages] * (1.0 / 2.0**22))
    return from_short(ref[:passages, :]) * (value_of(code[0:1, :]) * (1.0 / FULL)), square


def add_terms(terms):
    sumsq = functools.reduce(jnp.add, [square for _, square in terms])
    scale = lax.rsqrt(norm_of(sumsq))
    return functools.reduce(jnp.add, [value * turn(scale * jnp.sqrt(norm_of(square))) for value, square in terms]), sumsq


def add_body(score_ref, sumsq_ref, message_ref, out_ref):
    value, sumsq = add_terms([(score_ref[...], sumsq_ref[0:1, :]), read_scores(message_ref)])
    write_scores(value, sumsq, out_ref)


def add_scores(score, sumsq, message):
    return pl.pallas_call(
        add_body,
        in_specs=[VMEM] * 3,
        out_specs=VMEM,
        out_shape=jax.ShapeDtypeStruct(message.shape, message.dtype),
        compiler_params=params(8),
        name="add_scores",
    )(score, sumsq, message)


def half_of(value, half, owners):
    size = value.shape[0] // owners // 2
    return jnp.concatenate([value[(2 * n + half) * size:(2 * n + half + 1) * size] for n in range(owners)], axis=0)


def weight_body(owners, me_ref, owner_ref, own_ref, sumsq_ref, *rest):
    *messages, first_ref, second_ref = rest
    passages, rows = own_ref.shape
    value, _ = add_terms([(own_ref[...], sumsq_ref[0:1, :])] + [read_scores(message) for message in messages])
    score = value * (2.5 / math.sqrt(K))
    owner = owner_ref[:, pl.ds(pl.multiple_of(me_ref[0] * rows, rows), rows)]
    owned = owner == lax.broadcasted_iota(jnp.int32, (passages, rows), 0)
    score = jnp.where(owned, LOW, score)
    top = jnp.max(score, axis=1, keepdims=True)
    weight = jnp.where(owned, 0.0, jnp.exp(score - top))
    total = jnp.sum(weight, axis=1, keepdims=True)
    first_ref[:passages // 2, :] = half_of(weight, 0, owners).astype(BF16)
    first_ref[passages // 2:, :] = code_rows(split3(turn_back(top)) + split3(turn_back(total)), rows).astype(BF16)
    second_ref[...] = half_of(weight, 1, owners).astype(BF16)


def weights_of(me, owner, own, sumsq, messages, owners):
    passages, rows = own.shape
    return pl.pallas_call(
        functools.partial(weight_body, owners),
        grid_spec=pltpu.PrefetchScalarGridSpec(
            num_scalar_prefetch=1, grid=(), in_specs=[VMEM] * (3 + len(messages)), out_specs=[VMEM] * 2
        ),
        out_shape=[
            jax.ShapeDtypeStruct((passages // 2 + CODES, rows), BF16),
            jax.ShapeDtypeStruct((passages // 2, rows), BF16),
        ],
        compiler_params=params(8),
        cost_estimate=pl.CostEstimate(flops=8 * passages * rows, bytes_accessed=16 * passages * rows, transcendentals=passages * rows),
        name="weights",
    )(me, owner.reshape(1, -1), own, sumsq, *messages)


def running_stats(owners, codes, before):
    rows = 2 * (codes[0].shape[0] - CODES)
    codes = [code[code.shape[0] - CODES:, :rows].astype(F32) for code in codes]

    def columns(first):
        turned = [turn((c[first:first + 1] + c[first + 1:first + 2]) + c[first + 2:first + 3]) for c in codes]
        return [jnp.concatenate([half_of(column, half, owners) for half in range(2)], axis=0) for column in turned]

    tops, totals = columns(0), columns(3)
    if before is not None:
        tops.append(before[:, 0:1])
        totals.append(before[:, 1:2])
    top = functools.reduce(jnp.maximum, tops)
    factors = [jnp.exp(t - top) for t in tops]
    total = functools.reduce(jnp.add, [f * t for f, t in zip(factors, totals)])
    return top, total, factors


def add_sums(weights, quarters, factors, old, acc_ref):
    step = 512
    for n, (weight, quarter) in enumerate(zip(weights, quarters)):
        for at in range(0, acc_ref.shape[1], step):
            here = slice(at, at + step)
            value = factors[n] * jnp.dot(weight, quarter[:, here], preferred_element_type=F32)
            if n:
                value = acc_ref[:, here] + value
            elif old is not None:
                value = factors[-1] * old[:, here] + value
            acc_ref[:, here] = value


def stats_tile(top, total):
    lane = lax.broadcasted_iota(jnp.int32, (top.shape[0], LANES), 1)
    return jnp.where(lane == 0, top, total)


def sums_body(owners, sources, started, fetch, me_ref, *rest):
    count = 2 * sources
    parts, held_ref, rest = rest[:count], rest[count], rest[count + 1:]
    before, rest = rest[:2 * started], rest[2 * started:]
    if fetch:
        corpus_hbm, acc_ref, stats_ref, fetch_ref, sem = rest
        size = fetch_ref.shape[0]
        at = pl.multiple_of(sources_of(me_ref[0])[fetch] * size, size)
        load = pltpu.make_async_copy(corpus_hbm.at[pl.ds(at, size), :], fetch_ref, sem)
        load.start()
    else:
        acc_ref, stats_ref = rest[-2:]
    pieces = [parts[2 * n:2 * n + 2] for n in range(sources)]
    quarters = [held_ref] if sources == 1 else [held_ref.at[n] for n in range(sources)]
    top, total, factors = running_stats(owners, parts[::2], before[1] if before else None)
    weights = [jnp.concatenate([piece[0][:piece[1].shape[0], :], piece[1][...]], axis=0) for piece in pieces]
    add_sums(weights, quarters, factors, before[0] if before else None, acc_ref)
    stats_ref[...] = stats_tile(top, total)
    if fetch:
        load.wait()


def weighted_sums(me, owners, pieces, held, before, corpus=None, fetch=0, after=()):
    parts = [part for piece in pieces for part in piece]
    passages = 2 * parts[1].shape[0]
    quarter, depth = held.shape[-2:]
    fetched = [jax.ShapeDtypeStruct((quarter, depth), BF16)] if fetch else []
    return pl.pallas_call(
        functools.partial(sums_body, owners, len(pieces), len(before) // 2, fetch),
        grid_spec=pltpu.PrefetchScalarGridSpec(
            num_scalar_prefetch=1,
            grid=(),
            in_specs=[VMEM] * (len(parts) + 1 + len(before)) + [HBM] * len(fetched) + [ANY] * len(after),
            out_specs=[VMEM] * (2 + len(fetched)),
            scratch_shapes=[pltpu.SemaphoreType.DMA] * len(fetched),
        ),
        out_shape=[jax.ShapeDtypeStruct((passages, depth), F32), jax.ShapeDtypeStruct((passages, LANES), F32)] + fetched,
        compiler_params=params(30 if fetch else 8),
        cost_estimate=pl.CostEstimate(flops=2 * passages * quarter * len(pieces) * depth, bytes_accessed=2 * quarter * depth, transcendentals=0),
        name="weighted_sums",
    )(me, *parts, held, *before, *([corpus] if fetch else []), *after)


def last_sums_body(half, nrows, nsub, place_ref, piece_ref, held_ref, old_ref, stats_ref, *rest):
    send_ref, keep_ref = rest[:2] if half == 0 else rest[-3:-1]
    acc = rest[-1]
    span = send_ref.shape[1]
    passages, depth = acc.shape
    core = place_ref[1]
    if half == 0:
        top, total, factors = running_stats(nrows * nsub, [piece_ref], stats_ref)
        share = 1.0 / jnp.maximum(total, 1e-30)
        level = top + jnp.log(jnp.maximum(total, 1e-30))
        columns = [factors[0] * share, factors[1] * share, level]
        lane = lax.broadcasted_iota(jnp.int32, (passages, LANES), 1)
        later = [column[passages:] for column in columns]
        rest[2][...] = jnp.where(lane == 0, later[0], jnp.where(lane == 1, later[1], later[2]))
        columns = [column[:passages] for column in columns]
    else:
        columns = [stats_ref[:, n:n + 1] for n in range(3)]
    old = old_ref.at[pl.ds(half * passages, passages), :]
    add_sums([piece_ref[:passages, :]], [held_ref], columns[:2], old, acc)
    mine = [pl.multiple_of((x * nsub + core) * span, span) for x in range(nrows)]
    other = [pl.multiple_of((x * nsub + (nsub - 1 - core)) * span, span) for x in range(nrows)]
    for x in range(nrows):
        keep_ref[x, :, :depth] = acc[pl.ds(mine[x], span), :]
        send_ref[x, :, :depth] = acc[pl.ds(other[x], span), :].astype(BF16)
    acc[:, 0:LANES] = jnp.broadcast_to(columns[2], (passages, LANES))
    for x in range(nrows):
        keep_ref[x, :, depth:] = acc[pl.ds(mine[x], span), 0:LANES]
        send_ref[x, :, depth:] = pack_level(acc[pl.ds(other[x], span), 0:LANES])


def last_sums(place, half, piece, held, sums, stats, nrows, nsub):
    quarter, depth = held.shape
    passages = sums.shape[0] // 2
    shape = (nrows, passages // (nrows * nsub), depth + LANES)
    ratios = [jax.ShapeDtypeStruct((passages, LANES), F32)] * (1 - half)
    return pl.pallas_call(
        functools.partial(last_sums_body, half, nrows, nsub),
        grid_spec=pltpu.PrefetchScalarGridSpec(
            num_scalar_prefetch=1,
            grid=(),
            in_specs=[VMEM] * 4,
            out_specs=[VMEM] * (3 - half),
            scratch_shapes=[pltpu.VMEM((passages, depth), F32)],
        ),
        out_shape=[jax.ShapeDtypeStruct(shape, BF16), jax.ShapeDtypeStruct(shape, F32)] + ratios,
        compiler_params=params(),
        cost_estimate=pl.CostEstimate(flops=0, bytes_accessed=0, transcendentals=0),
        name="last_sums",
    )(place, piece, held, sums, stats)


def merge_shares(mine, other):
    top = jnp.maximum(mine, other)
    a, b = jnp.exp(mine - top), jnp.exp(other - top)
    share = 1.0 / (a + b)
    return a * share, b * share, top + jnp.log(a + b)


def merged(keep_ref, other_ref, a, b, tile):
    here = slice(tile * LANES, (tile + 1) * LANES)
    return keep_ref[:, here] * a + other_ref[:, here].astype(F32) * b


def merge_core_body(place_ref, keep_ref, other_ref, send_ref, next_ref):
    depth = send_ref.shape[1] - LANES
    mine = place_ref[2]
    blocks = [(keep_ref.at[at], other_ref.at[at]) for at in (1 - mine, mine)]
    shares = [merge_shares(keep[:, depth:], unpack_level(other[:, depth:])) for keep, other in blocks]
    for tile in range(depth // LANES):
        here = slice(tile * LANES, (tile + 1) * LANES)
        send_ref[:, here] = merged(*blocks[0], *shares[0][:2], tile).astype(BF16)
        next_ref[:, here] = merged(*blocks[1], *shares[1][:2], tile)
    send_ref[:, depth:] = pack_level(shares[0][2])
    next_ref[:, depth:] = shares[1][2]


def merge_core(place, keep, other):
    shape = keep.shape[1:]
    return pl.pallas_call(
        merge_core_body,
        grid_spec=pltpu.PrefetchScalarGridSpec(
            num_scalar_prefetch=1,
            grid=(),
            in_specs=[pl.BlockSpec(memory_space=pltpu.VMEM)] * 2,
            out_specs=[pl.BlockSpec(memory_space=pltpu.VMEM)] * 2,
        ),
        out_shape=[jax.ShapeDtypeStruct(shape, BF16), jax.ShapeDtypeStruct(shape, F32)],
        compiler_params=params(),
        name="merge_core",
    )(place, keep, other)


def merge_last_body(done, keep_ref, other_ref, *rest):
    out_ref = rest[-1]
    if done:
        out_ref[:done, :] = rest[0][...]
    depth = keep_ref.shape[1] - LANES
    a, b, _ = merge_shares(keep_ref[:, depth:], unpack_level(other_ref[:, depth:]))
    for tile in range(depth // LANES):
        out_ref[done:, tile * LANES:(tile + 1) * LANES] = merged(keep_ref, other_ref, a, b, tile)


def merge_last(keep, other, before):
    done = before[0].shape[0] if before else 0
    return pl.pallas_call(
        functools.partial(merge_last_body, done),
        in_specs=[VMEM] * (2 + len(before)),
        out_specs=VMEM,
        out_shape=jax.ShapeDtypeStruct((done + keep.shape[0], keep.shape[1] - LANES), F32),
        compiler_params=params(),
        name="merge_last",
    )(keep, other, *before)


def shift(value, axis, by):
    count = lax.axis_size(axis)
    return lax.ppermute(value, axis, [(i, (i + by) % count) for i in range(count)])


def scatter_parts(blocks):
    return [blocks[0]] + [shift(blocks[j], "feat", j) for j in range(1, len(blocks))]


def to_pair(value):
    return lax.ppermute(value, "feat", [(i, i ^ 1) for i in range(lax.axis_size("feat"))])


def sources_of(me):
    return [me, me ^ 1, me ^ 2, me ^ 3]


def relay_body(piece_ref, *rest):
    rest[-1][...] = piece_ref[...]


def relay(piece, *after):
    return pl.pallas_call(
        relay_body,
        in_specs=[VMEM] + [ANY] * len(after),
        out_specs=VMEM,
        out_shape=jax.ShapeDtypeStruct(piece.shape, piece.dtype),
        compiler_params=params(),
        name="relay",
    )(piece, *after)


def gather_tokens(me, g_own, g_others, piece, meanwhile):
    across, beside = shift(piece, "feat", 2), to_pair(piece)
    first = pack([piece, beside, across])
    g_low = join(join_g_body, [g_own] + g_others, (first,))
    last = pack([to_pair(across)], [g_low])
    done = meanwhile(last)
    width = g_low.shape[0]
    here = token_block(me, first, last, width)
    there = token_block(me, shift(first, "rows", 1), shift(last, "rows", 1), width, (done,))
    return [here, there, shift(here, "sub", 1), shift(there, "sub", 1)], [(0, 0), (1, 0), (0, 1), (1, 1)], done


def fast(activations, out_grads, proj_in, proj_out, lengths, corpus, owner):
    nfeat, nrows, nsub = (lax.axis_size(a) for a in ("feat", "rows", "sub"))
    feat, row, sub = (lax.axis_index(a).astype(jnp.int32) for a in ("feat", "rows", "sub"))
    me = feat.reshape(1)
    ends = jnp.cumsum(lengths)
    starts = ends - lengths
    x_parts = project_x(me, activations, proj_in, nfeat)
    g_parts = project_g(me, out_grads, proj_out, nfeat, starts, ends)
    x_piece = join(join_x_body, scatter_parts(x_parts), g_parts[:1])
    blocks, back, held_own = gather_tokens(
        me, g_parts[0], scatter_parts(g_parts)[1:], x_piece, lambda after: hold(me, corpus, nfeat, after)
    )
    order = [(row ^ d) * nsub + (sub ^ c) for d, c in back]
    place = jnp.stack([feat, sub, row] + order)
    message, sumsq, low, held = first_scores(place, starts, ends, blocks, corpus, nfeat)
    own, across, beside = near_scores(low, sumsq, held_own, held)
    across = add_scores(across, sumsq, to_pair(message))
    owners = nrows * nsub
    messages = [to_pair(beside), shift(across, "feat", 2)]
    pieces = weights_of(me, owner, own, sumsq, messages, owners)
    beside, across = [to_pair(p) for p in pieces], [shift(p, "feat", 2) for p in pieces]
    *sums, fetched = weighted_sums(me, owners, [pieces], held_own, (), corpus, 3)
    relayed = [relay(across[0], sums[1])]
    relayed.append(relay(across[1], relayed[0]))
    last = [to_pair(p) for p in relayed]
    sums = weighted_sums(me, owners, [beside, across], held, sums, after=relayed[1:])
    *first, ratios = last_sums(place, 0, last[0], fetched, *sums, nrows, nsub)
    halves = [first, last_sums(place, 1, last[1], fetched, sums[0], ratios, nrows, nsub)]
    ended = [merge_core(place, keep, shift(send, "sub", 1)) for send, keep in halves]
    out = ()
    for send, keep in ended:
        out = (merge_last(keep, shift(send, "rows", 1), out),)
    return out[0]


def general(activations, out_grads, proj_in, proj_out, lengths, corpus, owner):
    tok_local = activations.shape[0]
    passages = lengths.shape[0]
    nfeat = lax.axis_size("feat")
    part_x = jnp.dot(activations, proj_in, preferred_element_type=F32)
    part_g = jnp.dot(out_grads, proj_out, preferred_element_type=F32)
    width_cols = part_g.shape[1] // nfeat
    x_low = lax.psum(part_x, "feat").astype(BF16)
    g_low = lax.psum_scatter(part_g, "feat", scatter_dimension=1, tiled=True).astype(BF16)
    ends = jnp.cumsum(lengths)
    starts = ends - lengths
    positions = lax.axis_index(("rows", "sub")) * tok_local + jnp.arange(tok_local, dtype=jnp.int32)
    member = ((positions[None, :] >= starts[:, None]) & (positions[None, :] < ends[:, None])).astype(BF16)
    scaled_member = member[None, :, :] * jnp.transpose(g_low)[:, None, :]
    partial_grad = jnp.einsum("apt,tb->pab", scaled_member, x_low, preferred_element_type=F32)
    partial_grad = partial_grad.reshape(passages, width_cols * x_low.shape[1])
    pgrad = lax.psum(partial_grad, ("rows", "sub"))
    pgrad_low = pgrad.astype(BF16)
    sumsq_part = jnp.sum(pgrad * pgrad, axis=1)
    raw_part = lax.dot_general(pgrad_low, corpus, (((1,), (1,)), ((), ())), preferred_element_type=F32)
    labels = jnp.arange(passages, dtype=jnp.int32)[:, None]
    raw, sumsq = lax.psum((raw_part, sumsq_part), "feat")
    scale = 2.5 / math.sqrt(K) * lax.rsqrt(sumsq / K + 1e-06)
    score = raw * scale[:, None]
    owned = owner[None, :] == labels
    top = lax.pmax(jnp.max(jnp.where(owned, F32(LOW), score), axis=1), ("rows", "sub"))
    weight = jnp.where(owned, F32(0.0), jnp.exp(score - top[:, None]))
    total = lax.psum(jnp.sum(weight, axis=1), ("rows", "sub"))
    span = passages // lax.axis_size(("rows", "sub"))
    summed = lax.psum_scatter(
        jnp.dot(weight.astype(BF16), corpus, preferred_element_type=F32),
        ("rows", "sub"),
        scatter_dimension=0,
        tiled=True,
    )
    own_total = lax.dynamic_slice_in_dim(total, lax.axis_index(("rows", "sub")) * span, span, 0)
    return summed / own_total[:, None]


def solution(mesh):
    small = mesh.shape["feat"] == 4 and mesh.shape["rows"] == 2 and mesh.shape["sub"] == 2
    return jax.shard_map(
        fast if small else general,
        mesh=mesh,
        in_specs=(
            P(("groups", "rows", "sub"), "feat"),
            P(("groups", "rows", "sub"), "feat"),
            P(("groups", "feat"), None),
            P(("groups", "feat"), None),
            P("groups"),
            P(("groups", "rows", "sub"), "feat"),
            P(("rows", "sub")),
        ),
        out_specs=P(("groups", "rows", "sub"), "feat"),
        check_vma=False,
    )
```

```python
import functools
import math

import jax
import jax.numpy as jnp
from jax import lax
from jax.experimental import pallas as pl
from jax.experimental.pallas import tpu as pltpu
from jax.sharding import PartitionSpec as P

K = 16384
LONGEST = 64
LANES = 128
LOW = -1e30
F32, BF16 = jnp.float32, jnp.bfloat16
MIB = 1024 * 1024
CODES = 16
STEP = 369.0
FULL = 32767.0


def params(mib=16):
    return pltpu.CompilerParams(vmem_limit_bytes=mib * MIB)


def whole(shape):
    return pl.BlockSpec(shape, lambda *_: (0,) * len(shape))


VMEM = pl.BlockSpec(memory_space=pltpu.VMEM)
ANY = pl.BlockSpec(memory_space=pl.ANY)
HBM = pl.BlockSpec(memory_space=pltpu.HBM)


def level_of(value):
    return jnp.floor(jnp.log(jnp.maximum(value, 1e-30)) * STEP)


def value_of(level):
    return jnp.exp(level * (1.0 / STEP))


def to_short(value):
    return jnp.floor(value + 0.5).astype(jnp.int32).astype(jnp.int16)


def from_short(value):
    return value.astype(jnp.int32).astype(F32)


def scale_level(peak):
    return level_of(peak) + 2.0


def turned_dot(proj_t, tokens):
    return lax.dot_general(proj_t, tokens, (((1,), (1,)), ((), ())), preferred_element_type=F32)


def rows_of(total, count):
    return [pl.ds(n * (total // count), total // count) for n in range(count)]


def eye(size):
    return jnp.where(
        lax.broadcasted_iota(jnp.int32, (size, size), 0) == lax.broadcasted_iota(jnp.int32, (size, size), 1), 1.0, 0.0
    ).astype(BF16)


def turn_low(value):
    return turned_dot(eye(value.shape[1]), value).astype(BF16)


def x_body(nfeat, steps, ahead, me_ref, act_hbm, proj_hbm, own_ref, *rest):
    outs, (acts, proj, total, act_sems, proj_sems) = rest[:nfeat - 1], rest[nfeat - 1:]
    rank, quarter = own_ref.shape
    depth = proj_hbm.shape[0]
    chunks = rows_of(depth, steps)
    loads = [pltpu.make_async_copy(act_hbm.at[:, c], acts.at[n], act_sems.at[n]) for n, c in enumerate(chunks)]
    proj_loads = [pltpu.make_async_copy(proj_hbm.at[c, :], proj.at[n], proj_sems.at[n]) for n, c in enumerate(chunks)]
    for n in range(ahead):
        proj_loads[n].start()
        loads[n].start()
    for n in range(steps):
        proj_loads[n].wait()
        proj_t = turn_low(proj[n])
        loads[n].wait()
        if n + ahead < steps:
            proj_loads[n + ahead].start()
            loads[n + ahead].start()
        part = turned_dot(proj_t, acts[n])
        total[...] = part if n == 0 else total[...] + part
    for j in range(nfeat):
        to = lax.rem(me_ref[0] + j, nfeat)
        value = total[:, pl.ds(pl.multiple_of(to * quarter, quarter), quarter)]
        if j == 0:
            own_ref[...] = value
        else:
            level = scale_level(jnp.max(jnp.abs(value), axis=0, keepdims=True))
            outs[j - 1][:rank, :] = to_short(value * (FULL / value_of(level)))
            outs[j - 1][rank:, :] = jnp.broadcast_to(level, (CODES, quarter)).astype(jnp.int32).astype(jnp.int16)


def project_x(me, act, proj, nfeat):
    tok, depth = act.shape
    rank = proj.shape[1]
    quarter = tok // nfeat
    steps = 7
    chunk = depth // steps
    return pl.pallas_call(
        functools.partial(x_body, nfeat, steps, 3),
        grid_spec=pltpu.PrefetchScalarGridSpec(
            num_scalar_prefetch=1,
            grid=(),
            in_specs=[HBM, HBM],
            out_specs=[VMEM] * nfeat,
            scratch_shapes=[
                pltpu.VMEM((steps, tok, chunk), BF16),
                pltpu.VMEM((steps, chunk, rank), BF16),
                pltpu.VMEM((rank, tok), F32),
                pltpu.SemaphoreType.DMA((steps,)),
                pltpu.SemaphoreType.DMA((steps,)),
            ],
        ),
        out_shape=[jax.ShapeDtypeStruct((rank, quarter), F32)]
        + [jax.ShapeDtypeStruct((rank + CODES, quarter), jnp.int16)] * (nfeat - 1),
        compiler_params=params(52),
        cost_estimate=pl.CostEstimate(flops=2 * tok * depth * rank, bytes_accessed=2 * depth * (tok + rank), transcendentals=0),
        name="project_x",
    )(me, act, proj)


def g_body(nfeat, steps, me_ref, grad_hbm, proj_hbm, starts_ref, ends_ref, own_ref, *rest):
    outs, (grads, proj, turned, grad_sems, proj_sem) = rest[:nfeat - 1], rest[nfeat - 1:]
    width, tok = own_ref.shape
    rows = rows_of(tok, steps)
    proj_load = pltpu.make_async_copy(proj_hbm, proj, proj_sem)
    proj_load.start()
    loads = [pltpu.make_async_copy(grad_hbm.at[r, :], grads.at[r, :], grad_sems.at[n]) for n, r in enumerate(rows)]
    for load in loads:
        load.start()
    proj_load.wait()
    proj_t = turn_low(proj[...])
    for n in range(0, steps, 2):
        loads[n].wait()
        loads[n + 1].wait()
        at = slice(n * tok // steps, (n + 2) * tok // steps)
        turned[:, at] = turned_dot(proj_t, grads[at, :])
    chunks = tok // LANES
    for j in range(nfeat):
        to = lax.rem(me_ref[0] + j, nfeat)
        at = pl.ds(pl.multiple_of(to * width, width), width)
        if j == 0:
            own_ref[...] = turned[at, :]
        else:
            parts = [turned[at, n * LANES:(n + 1) * LANES] for n in range(chunks)]
            peak = functools.reduce(jnp.maximum, [jnp.abs(p) for p in parts])
            level = scale_level(jnp.max(peak, axis=0, keepdims=True))
            factor = FULL / value_of(level)
            for n in range(chunks):
                outs[j - 1][n * width:(n + 1) * width, :] = to_short(parts[n] * factor)
            outs[j - 1][chunks * width:, :] = jnp.broadcast_to(level, (CODES, LANES)).astype(jnp.int32).astype(jnp.int16)


def project_g(me, grads, proj, nfeat, *after):
    tok, depth = grads.shape
    rank = proj.shape[1]
    width = rank // nfeat
    steps = 4
    short = (tok // LANES * width + CODES, LANES)
    return pl.pallas_call(
        functools.partial(g_body, nfeat, steps),
        grid_spec=pltpu.PrefetchScalarGridSpec(
            num_scalar_prefetch=1,
            grid=(),
            in_specs=[HBM, HBM] + [ANY] * len(after),
            out_specs=[VMEM] * nfeat,
            scratch_shapes=[
                pltpu.VMEM((tok, depth), BF16),
                pltpu.VMEM((depth, rank), BF16),
                pltpu.VMEM((rank, tok), F32),
                pltpu.SemaphoreType.DMA((steps,)),
                pltpu.SemaphoreType.DMA,
            ],
        ),
        out_shape=[jax.ShapeDtypeStruct((width, tok), F32)] + [jax.ShapeDtypeStruct(short, jnp.int16)] * (nfeat - 1),
        compiler_params=params(53),
        cost_estimate=pl.CostEstimate(flops=2 * tok * depth * rank, bytes_accessed=2 * depth * (tok + rank), transcendentals=0),
        name="project_g",
    )(me, grads, proj, *after)


def join_x_body(nafter, *refs):
    own_ref, others, out_ref = refs[nafter], refs[nafter + 1:-1], refs[-1]
    rows = own_ref.shape[0]
    value = own_ref[...]
    for other in others:
        scale = value_of(from_short(other[rows:, :])[0:1, :]) * (1.0 / FULL)
        value = value + from_short(other[:rows, :]) * scale
    out_ref[...] = value.astype(BF16)


def join_g_body(nafter, *refs):
    own_ref, others, out_ref = refs[nafter], refs[nafter + 1:-1], refs[-1]
    width, tok = own_ref.shape
    chunks = tok // LANES
    scales = [value_of(from_short(other[chunks * width:, :])[0:1, :]) * (1.0 / FULL) for other in others]
    for c in range(chunks):
        value = own_ref[:, c * LANES:(c + 1) * LANES]
        for other, scale in zip(others, scales):
            value = value + from_short(other[c * width:(c + 1) * width, :]) * scale
        out_ref[:, c * LANES:(c + 1) * LANES] = value.astype(BF16)


def join(body, parts, after=()):
    return pl.pallas_call(
        functools.partial(body, len(after)),
        in_specs=[ANY] * len(after) + [VMEM] * len(parts),
        out_specs=VMEM,
        out_shape=jax.ShapeDtypeStruct(parts[0].shape, BF16),
        compiler_params=params(),
        name=body.__name__,
    )(*after, *parts)


def pack_body(x_refs, *rest):
    pieces, more, out_ref = rest[:x_refs], rest[x_refs:-1], rest[-1]
    size = pieces[0].shape[1]
    for n, piece in enumerate(pieces):
        out_ref[:, n * size:(n + 1) * size] = piece[...]
    for ref in more:
        rows = ref.shape[0]
        for n in range(ref.shape[1] // size):
            out_ref[n * rows:(n + 1) * rows, x_refs * size:] = ref[:, n * size:(n + 1) * size]


def pack(pieces, more=()):
    rows, size = pieces[0].shape
    count = len(pieces) + len(more)
    return pl.pallas_call(
        functools.partial(pack_body, len(pieces)),
        in_specs=[VMEM] * count,
        out_specs=VMEM,
        out_shape=jax.ShapeDtypeStruct((rows, count * size), BF16),
        compiler_params=params(),
        name="pack",
    )(*pieces, *more)


def token_body(width, me_ref, first_ref, last_ref, out_ref):
    rank = first_ref.shape[0]
    size = last_ref.shape[1] // 2
    pieces = [first_ref[:, n * size:(n + 1) * size] for n in range(3)] + [last_ref[:, :size]]
    for source, piece in zip(sources_of(me_ref[0]), pieces):
        out_ref[:rank, pl.ds(pl.multiple_of(source * size, size), size)] = piece
    for n in range(rank // width):
        out_ref[rank:, n * size:(n + 1) * size] = last_ref[n * width:(n + 1) * width, size:]


def token_block(me, first, last, width):
    rank, size = last.shape
    return pl.pallas_call(
        functools.partial(token_body, width),
        grid_spec=pltpu.PrefetchScalarGridSpec(
            num_scalar_prefetch=1, grid=(), in_specs=[VMEM] * 2, out_specs=VMEM
        ),
        out_shape=jax.ShapeDtypeStruct((rank + width, rank // width * size // 2), BF16),
        compiler_params=params(),
        name="token_block",
    )(me, first, last)


def turn(row):
    return jnp.transpose(jnp.broadcast_to(row, (LANES, row.shape[1])))[:, 0:1]


def turn_back(column):
    return jnp.transpose(jnp.broadcast_to(column, (column.shape[0], LANES)))[0:1, :]


def norm_of(sumsq):
    return sumsq / K + 1e-06


def spread(row, lanes):
    return jnp.concatenate([row] * (lanes // row.shape[1]), axis=1)


def code_rows(rows, lanes):
    at = lax.broadcasted_iota(jnp.int32, (CODES, lanes), 0)
    tile = jnp.zeros((CODES, lanes), F32)
    for n, row in enumerate(rows):
        tile = jnp.where(at == n, spread(row, lanes), tile)
    return tile


def loads_of(corpus_hbm, corpus_ref, sems, quarters, halves):
    size = corpus_ref.shape[1]
    loads = []
    for n, quarter in enumerate(quarters):
        rows = pl.ds(pl.multiple_of(quarter * size, size), size)
        for h, here in enumerate(rows_of(corpus_ref.shape[2], halves)):
            loads.append(pltpu.make_async_copy(corpus_hbm.at[rows, here], corpus_ref.at[n, :, here], sems.at[n * halves + h]))
    return loads


def write_scores(value, sumsq, out_ref):
    passages, quarter = value.shape
    coarse = level_of(sumsq)
    fine = jnp.floor((jnp.maximum(sumsq, 1e-30) / value_of(coarse) - 1.0) * (2.0**22))
    level = scale_level(jnp.max(jnp.abs(value), axis=0, keepdims=True))
    out_ref[:passages, :] = to_short(value * (FULL / value_of(level)))
    out_ref[passages:, :] = code_rows([level, coarse, fine], quarter).astype(jnp.int32).astype(jnp.int16)


def first_body(nblk, passages, place_ref, starts_ref, ends_ref, *rest):
    blocks, corpus_hbm = rest[:nblk], rest[nblk]
    out_ref, sumsq_ref, low, held_ref, corpus_ref, tokens, grad, sems, held_sems = rest[nblk + 1:]
    me = place_ref[0]
    sources = sources_of(me)
    loads = loads_of(corpus_hbm, corpus_ref, sems, sources[3:], 1)
    later = loads_of(corpus_hbm, held_ref, held_sems, sources[1:3], 1)
    for load in loads + later:
        load.start()

    height, tok = blocks[0].shape
    rank = height - low.shape[1] // LANES
    width = height - rank
    for n in range(nblk):
        tokens[:, pl.ds(pl.multiple_of(place_ref[3 + n] * tok, tok), tok)] = blocks[n][...]
    group = 8
    window = -(-group * LONGEST // LANES) * LANES + LANES

    def step(i, carry):
        first = pl.multiple_of(i * group, group)
        base = jnp.minimum((starts_ref[first] // LANES) * LANES, nblk * tok - window)
        here = pl.ds(pl.multiple_of(base, LANES), window)
        token = base + lax.broadcasted_iota(jnp.int32, (group, window), 1)
        row = lax.broadcasted_iota(jnp.int32, (group, window), 0)
        start = jnp.zeros((group, window), jnp.int32)
        end = start
        for q in range(group):
            start = jnp.where(row == q, starts_ref[first + q], start)
            end = jnp.where(row == q, ends_ref[first + q], end)
        member = jnp.where((token >= start) & (token < end), 1.0, 0.0)
        terms = tokens[rank:, here].astype(F32)[:, None, :] * member[None, :, :]
        product = turned_dot(terms.reshape(width * group, window).astype(BF16), tokens[:rank, here])
        grad[:, pl.ds(first, group), :] = product.reshape(width, group, rank)
        return carry

    lax.fori_loop(0, passages // group, step, 0, unroll=2)
    squares = jnp.zeros((passages, LANES), F32)
    for a in range(width):
        column = grad[a]
        squares = squares + column * column
        low[:, a * LANES:(a + 1) * LANES] = column.astype(BF16)
    sumsq = jnp.sum(jnp.transpose(squares), axis=0, keepdims=True)
    sumsq_ref[...] = jnp.broadcast_to(sumsq, sumsq_ref.shape)
    norm = turn(lax.rsqrt(norm_of(sumsq)))
    for load in loads:
        load.wait()
    write_scores(norm * turned_dot(low[...], corpus_ref[0]), sumsq, out_ref)
    for load in later:
        load.wait()


def first_scores(place, starts, ends, blocks, corpus, nfeat):
    passages = starts.shape[0]
    rows, depth = corpus.shape
    quarter = rows // nfeat
    height, tok = blocks[0].shape
    nblk = len(blocks)
    return pl.pallas_call(
        functools.partial(first_body, nblk, passages),
        grid_spec=pltpu.PrefetchScalarGridSpec(
            num_scalar_prefetch=3,
            grid=(),
            in_specs=[VMEM] * nblk + [HBM],
            out_specs=[VMEM] * 4,
            scratch_shapes=[
                pltpu.VMEM((1, quarter, depth), BF16),
                pltpu.VMEM((height, nblk * tok), BF16),
                pltpu.VMEM((depth // LANES, passages, LANES), F32),
                pltpu.SemaphoreType.DMA((1,)),
                pltpu.SemaphoreType.DMA((nfeat - 2,)),
            ],
        ),
        out_shape=[
            jax.ShapeDtypeStruct((passages + CODES, quarter), jnp.int16),
            jax.ShapeDtypeStruct((8, passages), F32),
            jax.ShapeDtypeStruct((passages, depth), BF16),
            jax.ShapeDtypeStruct((nfeat - 2, quarter, depth), BF16),
        ],
        compiler_params=params(30),
        cost_estimate=pl.CostEstimate(flops=2 * passages * depth * rows, bytes_accessed=rows * depth, transcendentals=0),
        name="first_scores",
    )(place, starts, ends, *blocks, corpus)


def near_body(low_ref, sumsq_ref, held_ref, across_ref, beside_ref):
    sumsq = sumsq_ref[0:1, :]
    norm = turn(lax.rsqrt(norm_of(sumsq)))
    write_scores(norm * turned_dot(low_ref[...], held_ref[0]), sumsq, beside_ref)
    across_ref[...] = norm * turned_dot(low_ref[...], held_ref[1])


def near_scores(low, sumsq, held):
    passages, depth = low.shape
    quarter = held.shape[1]
    return pl.pallas_call(
        near_body,
        in_specs=[VMEM] * 3,
        out_specs=[VMEM] * 2,
        out_shape=[
            jax.ShapeDtypeStruct((passages, quarter), F32),
            jax.ShapeDtypeStruct((passages + CODES, quarter), jnp.int16),
        ],
        compiler_params=params(8),
        cost_estimate=pl.CostEstimate(flops=4 * passages * depth * quarter, bytes_accessed=4 * quarter * depth, transcendentals=0),
        name="near_scores",
    )(low, sumsq, held)


def own_body(me_ref, low_ref, sumsq_ref, corpus_hbm, after_ref, own_ref, held_ref, sems):
    sources = sources_of(me_ref[0])
    loads = loads_of(corpus_hbm, held_ref, sems, [sources[0], sources[3]], 1)
    for load in loads:
        load.start()
    norm = turn(lax.rsqrt(norm_of(sumsq_ref[0:1, :])))
    loads[0].wait()
    own_ref[...] = norm * turned_dot(low_ref[...], held_ref[0])
    loads[1].wait()


def own_scores(me, low, sumsq, corpus, nfeat, after):
    passages, depth = low.shape
    quarter = corpus.shape[0] // nfeat
    return pl.pallas_call(
        own_body,
        grid_spec=pltpu.PrefetchScalarGridSpec(
            num_scalar_prefetch=1,
            grid=(),
            in_specs=[VMEM] * 2 + [HBM, ANY],
            out_specs=[VMEM] * 2,
            scratch_shapes=[pltpu.SemaphoreType.DMA((2,))],
        ),
        out_shape=[jax.ShapeDtypeStruct((passages, quarter), F32), jax.ShapeDtypeStruct((2, quarter, depth), BF16)],
        compiler_params=params(30),
        cost_estimate=pl.CostEstimate(flops=2 * passages * depth * quarter, bytes_accessed=4 * quarter * depth, transcendentals=0),
        name="own_scores",
    )(me, low, sumsq, corpus, after)


def open_body(message_ref, after_ref, score_ref, sumsq_ref):
    score_ref[...], sumsq = read_scores(message_ref)
    sumsq_ref[...] = jnp.broadcast_to(sumsq, sumsq_ref.shape)


def open_scores(message, after):
    passages, size = message.shape[0] - CODES, message.shape[1]
    return pl.pallas_call(
        open_body,
        in_specs=[VMEM, ANY],
        out_specs=[VMEM] * 2,
        out_shape=[jax.ShapeDtypeStruct((passages, size), F32), jax.ShapeDtypeStruct((8, passages), F32)],
        compiler_params=params(8),
        name="open_scores",
    )(message, after)


def split3(value):
    high = value.astype(BF16)
    rest = value - high.astype(F32)
    middle = rest.astype(BF16)
    return [p.astype(F32) for p in (high, middle, (rest - middle.astype(F32)).astype(BF16))]


def pack_level(tile):
    lane = lax.broadcasted_iota(jnp.int32, tile.shape, 1)
    out = jnp.zeros(tile.shape, F32)
    for n, piece in enumerate(split3(tile)):
        out = jnp.where(lane == n, piece, out)
    return out.astype(BF16)


def unpack_level(tile):
    return jnp.broadcast_to(jnp.sum(tile.astype(F32), axis=1, keepdims=True), tile.shape)


def read_scores(ref):
    passages = ref.shape[0] - CODES
    code = from_short(ref[passages:, :])
    base = value_of(code[1:2, :passages])
    square = base + base * (code[2:3, :passages] * (1.0 / 2.0**22))
    return from_short(ref[:passages, :]) * (value_of(code[0:1, :]) * (1.0 / FULL)), square


def add_terms(terms):
    sumsq = functools.reduce(jnp.add, [square for _, square in terms])
    scale = lax.rsqrt(norm_of(sumsq))
    return functools.reduce(jnp.add, [value * turn(scale * jnp.sqrt(norm_of(square))) for value, square in terms]), sumsq


def add_body(score_ref, sumsq_ref, message_ref, out_ref):
    value, sumsq = add_terms([(score_ref[...], sumsq_ref[0:1, :]), read_scores(message_ref)])
    write_scores(value, sumsq, out_ref)


def add_scores(score, sumsq, message):
    return pl.pallas_call(
        add_body,
        in_specs=[VMEM] * 3,
        out_specs=VMEM,
        out_shape=jax.ShapeDtypeStruct(message.shape, message.dtype),
        compiler_params=params(8),
        name="add_scores",
    )(score, sumsq, message)


def half_of(value, half, owners):
    size = value.shape[0] // owners // 2
    return jnp.concatenate([value[(2 * n + half) * size:(2 * n + half + 1) * size] for n in range(owners)], axis=0)


def weight_body(owners, me_ref, owner_ref, own_ref, sumsq_ref, open_ref, open_sumsq_ref, message_ref, first_ref, second_ref, whole_ref):
    passages, rows = own_ref.shape
    opened = open_ref[...], open_sumsq_ref[0:1, :]
    value, _ = add_terms([(own_ref[...], sumsq_ref[0:1, :]), opened, read_scores(message_ref)])
    score = value * (2.5 / math.sqrt(K))
    owner = owner_ref[:, pl.ds(pl.multiple_of(me_ref[0] * rows, rows), rows)]
    owned = owner == lax.broadcasted_iota(jnp.int32, (passages, rows), 0)
    score = jnp.where(owned, LOW, score)
    top = jnp.max(score, axis=1, keepdims=True)
    weight = jnp.where(owned, 0.0, jnp.exp(score - top))
    total = jnp.sum(weight, axis=1, keepdims=True)
    first_ref[:passages // 2, :] = half_of(weight, 0, owners).astype(BF16)
    first_ref[passages // 2:, :] = code_rows(split3(turn_back(top)) + split3(turn_back(total)), rows).astype(BF16)
    second_ref[...] = half_of(weight, 1, owners).astype(BF16)
    size = first_ref.shape[0]
    whole_ref[:size, :] = first_ref[...]
    whole_ref[size:, :] = second_ref[...]


def weights_of(me, owner, own, sumsq, opened, message, owners):
    passages, rows = own.shape
    return pl.pallas_call(
        functools.partial(weight_body, owners),
        grid_spec=pltpu.PrefetchScalarGridSpec(
            num_scalar_prefetch=1, grid=(), in_specs=[VMEM] * 6, out_specs=[VMEM] * 3
        ),
        out_shape=[
            jax.ShapeDtypeStruct((passages // 2 + CODES, rows), BF16),
            jax.ShapeDtypeStruct((passages // 2, rows), BF16),
            jax.ShapeDtypeStruct((passages + CODES, rows), BF16),
        ],
        compiler_params=params(8),
        cost_estimate=pl.CostEstimate(flops=8 * passages * rows, bytes_accessed=16 * passages * rows, transcendentals=passages * rows),
        name="weights",
    )(me, owner.reshape(1, -1), own, sumsq, *opened, message)


def running_stats(owners, codes, before):
    rows = 2 * (codes[0].shape[0] - CODES)
    codes = [code[code.shape[0] - CODES:, :rows].astype(F32) for code in codes]

    def columns(first):
        turned = [turn((c[first:first + 1] + c[first + 1:first + 2]) + c[first + 2:first + 3]) for c in codes]
        return [jnp.concatenate([half_of(column, half, owners) for half in range(2)], axis=0) for column in turned]

    tops, totals = columns(0), columns(3)
    if before is not None:
        tops.append(before[:, 0:1])
        totals.append(before[:, 1:2])
    top = functools.reduce(jnp.maximum, tops)
    factors = [jnp.exp(t - top) for t in tops]
    total = functools.reduce(jnp.add, [f * t for f, t in zip(factors, totals)])
    return top, total, factors


def add_sums(weights, quarters, factors, old, acc_ref):
    step = 512
    for n, (weight, quarter) in enumerate(zip(weights, quarters)):
        for at in range(0, acc_ref.shape[1], step):
            here = slice(at, at + step)
            value = factors[n] * jnp.dot(weight, quarter[:, here], preferred_element_type=F32)
            if n:
                value = acc_ref[:, here] + value
            elif old is not None:
                value = factors[-1] * old[:, here] + value
            acc_ref[:, here] = value


def stats_tile(top, total):
    lane = lax.broadcasted_iota(jnp.int32, (top.shape[0], LANES), 1)
    return jnp.where(lane == 0, top, total)


def sums_body(owners, counts, started, *rest):
    pieces = []
    for count in counts:
        parts, rest = rest[:count], rest[count:]
        if count == 1:
            size = (parts[0].shape[0] - CODES) // 2
            parts = parts[0].at[pl.ds(0, size + CODES), :], parts[0].at[pl.ds(size + CODES, size), :]
        pieces.append(parts)
    held_ref, rest = rest[0], rest[1:]
    before, acc_ref, stats_ref = rest[:2 * started], *rest[-2:]
    quarters = [held_ref.at[n] for n in range(len(counts))]
    codes = [piece[0] for piece in pieces]
    top, total, factors = running_stats(owners, codes, before[1] if before else None)
    weights = [jnp.concatenate([piece[0][:piece[1].shape[0], :], piece[1][...]], axis=0) for piece in pieces]
    add_sums(weights, quarters, factors, before[0] if before else None, acc_ref)
    stats_ref[...] = stats_tile(top, total)


def weighted_sums(owners, pieces, held, before, after=()):
    parts = [part for piece in pieces for part in piece]
    passages = 2 * pieces[-1][1].shape[0]
    _, quarter, depth = held.shape
    return pl.pallas_call(
        functools.partial(sums_body, owners, tuple(len(piece) for piece in pieces), len(before) // 2),
        in_specs=[VMEM] * (len(parts) + 1 + len(before)) + [ANY] * len(after),
        out_specs=[VMEM] * 2,
        out_shape=[jax.ShapeDtypeStruct((passages, depth), F32), jax.ShapeDtypeStruct((passages, LANES), F32)],
        compiler_params=params(8),
        cost_estimate=pl.CostEstimate(flops=2 * passages * quarter * len(pieces) * depth, bytes_accessed=2 * quarter * depth, transcendentals=0),
        name="weighted_sums",
    )(*parts, held, *before, *after)


def last_sums_body(half, nrows, nsub, place_ref, piece_ref, held_ref, old_ref, stats_ref, *rest):
    send_ref, keep_ref, later_ref, columns_ref = rest if half == 0 else rest[:2] + (None, rest[2])
    span = send_ref.shape[1]
    depth = held_ref.shape[2]
    passages = columns_ref.shape[0]
    core = place_ref[1]
    if half == 0:
        top, total, factors = running_stats(nrows * nsub, [piece_ref], stats_ref)
        share = 1.0 / jnp.maximum(total, 1e-30)
        level = top + jnp.log(jnp.maximum(total, 1e-30))
        columns = [factors[0] * share, factors[1] * share, level]
        lane = lax.broadcasted_iota(jnp.int32, (2 * passages, LANES), 1)
        tile = jnp.where(lane == 0, columns[0], jnp.where(lane == 1, columns[1], columns[2]))
        columns_ref[...] = tile[:passages]
        later_ref[...] = tile[passages:]
    else:
        columns_ref[...] = stats_ref[...]
    starts = [x * nsub + (nsub - 1 - core) for x in range(nrows)] + [x * nsub + core for x in range(nrows)]
    rows = [pl.ds(pl.multiple_of(n * span, span), span) for n in starts]
    old_rows = [pl.ds(pl.multiple_of(half * passages + n * span, span), span) for n in starts]
    weight = jnp.concatenate([piece_ref[r, :] for r in rows], axis=0)
    columns = jnp.concatenate([columns_ref[r, :] for r in rows], axis=0)
    new_factor, old_factor, level = columns[:, 0:1], columns[:, 1:2], columns[:, 2:3]
    step = 512
    for at in range(0, depth, step):
        here = slice(at, at + step)
        old = jnp.concatenate([old_ref[r, here] for r in old_rows], axis=0)
        value = new_factor * jnp.dot(weight, held_ref[1, :, here], preferred_element_type=F32) + old_factor * old
        for x in range(nrows):
            send_ref[x, :, here] = value[x * span:(x + 1) * span].astype(BF16)
            keep_ref[x, :, here] = value[(nrows + x) * span:(nrows + x + 1) * span]
    level = jnp.broadcast_to(level, (passages, LANES))
    for x in range(nrows):
        send_ref[x, :, depth:] = pack_level(level[x * span:(x + 1) * span])
        keep_ref[x, :, depth:] = level[(nrows + x) * span:(nrows + x + 1) * span]


def last_sums(place, half, piece, held, sums, stats, nrows, nsub):
    _, quarter, depth = held.shape
    passages = sums.shape[0] // 2
    shape = (nrows, passages // (nrows * nsub), depth + LANES)
    ratios = [jax.ShapeDtypeStruct((passages, LANES), F32)] * (1 - half)
    return pl.pallas_call(
        functools.partial(last_sums_body, half, nrows, nsub),
        grid_spec=pltpu.PrefetchScalarGridSpec(
            num_scalar_prefetch=1,
            grid=(),
            in_specs=[VMEM] * 4,
            out_specs=[VMEM] * (3 - half),
            scratch_shapes=[pltpu.VMEM((passages, LANES), F32)],
        ),
        out_shape=[jax.ShapeDtypeStruct(shape, BF16), jax.ShapeDtypeStruct(shape, F32)] + ratios,
        compiler_params=params(),
        cost_estimate=pl.CostEstimate(flops=0, bytes_accessed=0, transcendentals=0),
        name="last_sums",
    )(place, piece, held, sums, stats)


def merge_shares(mine, other):
    top = jnp.maximum(mine, other)
    a, b = jnp.exp(mine - top), jnp.exp(other - top)
    share = 1.0 / (a + b)
    return a * share, b * share, top + jnp.log(a + b)


def merged(keep_ref, other_ref, a, b, tile):
    here = slice(tile * LANES, (tile + 1) * LANES)
    return keep_ref[:, here] * a + other_ref[:, here].astype(F32) * b


def merge_core_body(place_ref, keep_ref, other_ref, send_ref, next_ref):
    depth = send_ref.shape[1] - LANES
    mine = place_ref[2]
    blocks = [(keep_ref.at[at], other_ref.at[at]) for at in (1 - mine, mine)]
    shares = [merge_shares(keep[:, depth:], unpack_level(other[:, depth:])) for keep, other in blocks]
    for tile in range(depth // LANES):
        here = slice(tile * LANES, (tile + 1) * LANES)
        send_ref[:, here] = merged(*blocks[0], *shares[0][:2], tile).astype(BF16)
        next_ref[:, here] = merged(*blocks[1], *shares[1][:2], tile)
    send_ref[:, depth:] = pack_level(shares[0][2])
    next_ref[:, depth:] = shares[1][2]


def merge_core(place, keep, other):
    shape = keep.shape[1:]
    return pl.pallas_call(
        merge_core_body,
        grid_spec=pltpu.PrefetchScalarGridSpec(
            num_scalar_prefetch=1,
            grid=(),
            in_specs=[pl.BlockSpec(memory_space=pltpu.VMEM)] * 2,
            out_specs=[pl.BlockSpec(memory_space=pltpu.VMEM)] * 2,
        ),
        out_shape=[jax.ShapeDtypeStruct(shape, BF16), jax.ShapeDtypeStruct(shape, F32)],
        compiler_params=params(),
        name="merge_core",
    )(place, keep, other)


def merge_last_body(done, keep_ref, other_ref, *rest):
    out_ref = rest[-1]
    if done:
        out_ref[:done, :] = rest[0][...]
    depth = keep_ref.shape[1] - LANES
    a, b, _ = merge_shares(keep_ref[:, depth:], unpack_level(other_ref[:, depth:]))
    for tile in range(depth // LANES):
        out_ref[done:, tile * LANES:(tile + 1) * LANES] = merged(keep_ref, other_ref, a, b, tile)


def merge_last(keep, other, before):
    done = before[0].shape[0] if before else 0
    return pl.pallas_call(
        functools.partial(merge_last_body, done),
        in_specs=[VMEM] * (2 + len(before)),
        out_specs=VMEM,
        out_shape=jax.ShapeDtypeStruct((done + keep.shape[0], keep.shape[1] - LANES), F32),
        compiler_params=params(),
        name="merge_last",
    )(keep, other, *before)


def shift(value, axis, by):
    count = lax.axis_size(axis)
    return lax.ppermute(value, axis, [(i, (i + by) % count) for i in range(count)])


def scatter_parts(blocks):
    return [blocks[0]] + [shift(blocks[j], "feat", j) for j in range(1, len(blocks))]


def to_pair(value):
    return lax.ppermute(value, "feat", [(i, i ^ 1) for i in range(lax.axis_size("feat"))])


def sources_of(me):
    return [me, me ^ 1, me ^ 2, me ^ 3]


def relay_body(piece_ref, *rest):
    rest[-1][...] = piece_ref[...]


def relay(piece, *after):
    return pl.pallas_call(
        relay_body,
        in_specs=[VMEM] + [ANY] * len(after),
        out_specs=VMEM,
        out_shape=jax.ShapeDtypeStruct(piece.shape, piece.dtype),
        compiler_params=params(),
        name="relay",
    )(piece, *after)


def gather_tokens(me, g_own, g_others, piece):
    across, beside = shift(piece, "feat", 2), to_pair(piece)
    first = pack([piece, beside, across])
    g_low = join(join_g_body, [g_own] + g_others, (first,))
    last = pack([to_pair(across)], [g_low])
    width = g_low.shape[0]
    here = token_block(me, first, last, width)
    there = token_block(me, shift(first, "rows", 1), shift(last, "rows", 1), width)
    return [here, there, shift(here, "sub", 1), shift(there, "sub", 1)], [(0, 0), (1, 0), (0, 1), (1, 1)]


def fast(activations, out_grads, proj_in, proj_out, lengths, corpus, owner):
    nfeat, nrows, nsub = (lax.axis_size(a) for a in ("feat", "rows", "sub"))
    feat, row, sub = (lax.axis_index(a).astype(jnp.int32) for a in ("feat", "rows", "sub"))
    me = feat.reshape(1)
    ends = jnp.cumsum(lengths)
    starts = ends - lengths
    x_parts = project_x(me, activations, proj_in, nfeat)
    g_parts = project_g(me, out_grads, proj_out, nfeat, starts, ends)
    x_piece = join(join_x_body, scatter_parts(x_parts), g_parts[:1])
    blocks, back = gather_tokens(me, g_parts[0], scatter_parts(g_parts)[1:], x_piece)
    order = [(row ^ d) * nsub + (sub ^ c) for d, c in back]
    place = jnp.stack([feat, sub, row] + order)
    message, sumsq, low, held = first_scores(place, starts, ends, blocks, corpus, nfeat)
    across, beside = near_scores(low, sumsq, held)
    across = add_scores(across, sumsq, to_pair(message))
    own, held_far = own_scores(me, low, sumsq, corpus, nfeat, across)
    owners = nrows * nsub
    opened = open_scores(to_pair(beside), own)
    *pieces, whole_piece = weights_of(me, owner, own, sumsq, opened, shift(across, "feat", 2), owners)
    across, beside = [shift(p, "feat", 2) for p in pieces], [to_pair(whole_piece)]
    sums = weighted_sums(owners, [pieces], held_far, ())
    relayed = [relay(across[0], sums[1])]
    relayed.append(relay(across[1], relayed[0]))
    last = [to_pair(p) for p in relayed]
    sums = weighted_sums(owners, [beside, across], held, sums, after=relayed[1:])
    *first, ratios = last_sums(place, 0, last[0], held_far, *sums, nrows, nsub)
    halves = [first, last_sums(place, 1, last[1], held_far, sums[0], ratios, nrows, nsub)]
    ended = [merge_core(place, keep, shift(send, "sub", 1)) for send, keep in halves]
    out = ()
    for send, keep in ended:
        out = (merge_last(keep, shift(send, "rows", 1), out),)
    return out[0]


def general(activations, out_grads, proj_in, proj_out, lengths, corpus, owner):
    tok_local = activations.shape[0]
    passages = lengths.shape[0]
    nfeat = lax.axis_size("feat")
    part_x = jnp.dot(activations, proj_in, preferred_element_type=F32)
    part_g = jnp.dot(out_grads, proj_out, preferred_element_type=F32)
    width_cols = part_g.shape[1] // nfeat
    x_low = lax.psum(part_x, "feat").astype(BF16)
    g_low = lax.psum_scatter(part_g, "feat", scatter_dimension=1, tiled=True).astype(BF16)
    ends = jnp.cumsum(lengths)
    starts = ends - lengths
    positions = lax.axis_index(("rows", "sub")) * tok_local + jnp.arange(tok_local, dtype=jnp.int32)
    member = ((positions[None, :] >= starts[:, None]) & (positions[None, :] < ends[:, None])).astype(BF16)
    scaled_member = member[None, :, :] * jnp.transpose(g_low)[:, None, :]
    partial_grad = jnp.einsum("apt,tb->pab", scaled_member, x_low, preferred_element_type=F32)
    partial_grad = partial_grad.reshape(passages, width_cols * x_low.shape[1])
    pgrad = lax.psum(partial_grad, ("rows", "sub"))
    pgrad_low = pgrad.astype(BF16)
    sumsq_part = jnp.sum(pgrad * pgrad, axis=1)
    raw_part = lax.dot_general(pgrad_low, corpus, (((1,), (1,)), ((), ())), preferred_element_type=F32)
    labels = jnp.arange(passages, dtype=jnp.int32)[:, None]
    raw, sumsq = lax.psum((raw_part, sumsq_part), "feat")
    scale = 2.5 / math.sqrt(K) * lax.rsqrt(sumsq / K + 1e-06)
    score = raw * scale[:, None]
    owned = owner[None, :] == labels
    top = lax.pmax(jnp.max(jnp.where(owned, F32(LOW), score), axis=1), ("rows", "sub"))
    weight = jnp.where(owned, F32(0.0), jnp.exp(score - top[:, None]))
    total = lax.psum(jnp.sum(weight, axis=1), ("rows", "sub"))
    span = passages // lax.axis_size(("rows", "sub"))
    summed = lax.psum_scatter(
        jnp.dot(weight.astype(BF16), corpus, preferred_element_type=F32),
        ("rows", "sub"),
        scatter_dimension=0,
        tiled=True,
    )
    own_total = lax.dynamic_slice_in_dim(total, lax.axis_index(("rows", "sub")) * span, span, 0)
    return summed / own_total[:, None]


def solution(mesh):
    small = mesh.shape["feat"] == 4 and mesh.shape["rows"] == 2 and mesh.shape["sub"] == 2
    return jax.shard_map(
        fast if small else general,
        mesh=mesh,
        in_specs=(
            P(("groups", "rows", "sub"), "feat"),
            P(("groups", "rows", "sub"), "feat"),
            P(("groups", "feat"), None),
            P(("groups", "feat"), None),
            P("groups"),
            P(("groups", "rows", "sub"), "feat"),
            P(("rows", "sub")),
        ),
        out_specs=P(("groups", "rows", "sub"), "feat"),
        check_vma=False,
    )
```

```python
import functools
import math

import jax
import jax.numpy as jnp
from jax import lax
from jax.experimental import pallas as pl
from jax.experimental.pallas import tpu as pltpu
from jax.sharding import PartitionSpec as P

K = 16384
LONGEST = 64
LANES = 128
LOW = -1e30
F32, BF16 = jnp.float32, jnp.bfloat16
MIB = 1024 * 1024
CODES = 16
STEP = 369.0
FULL = 32767.0


def params(mib=16):
    return pltpu.CompilerParams(vmem_limit_bytes=mib * MIB)


def whole(shape):
    return pl.BlockSpec(shape, lambda *_: (0,) * len(shape))


VMEM = pl.BlockSpec(memory_space=pltpu.VMEM)
ANY = pl.BlockSpec(memory_space=pl.ANY)
HBM = pl.BlockSpec(memory_space=pltpu.HBM)


def level_of(value):
    return jnp.floor(jnp.log(jnp.maximum(value, 1e-30)) * STEP)


def value_of(level):
    return jnp.exp(level * (1.0 / STEP))


def to_short(value):
    return jnp.floor(value + 0.5).astype(jnp.int32).astype(jnp.int16)


def from_short(value):
    return value.astype(jnp.int32).astype(F32)


def scale_level(peak):
    return level_of(peak) + 2.0


def turned_dot(proj_t, tokens):
    return lax.dot_general(proj_t, tokens, (((1,), (1,)), ((), ())), preferred_element_type=F32)


def rows_of(total, count):
    return [pl.ds(n * (total // count), total // count) for n in range(count)]


def eye(size):
    return jnp.where(
        lax.broadcasted_iota(jnp.int32, (size, size), 0) == lax.broadcasted_iota(jnp.int32, (size, size), 1), 1.0, 0.0
    ).astype(BF16)


def turn_low(value):
    return turned_dot(eye(value.shape[1]), value).astype(BF16)


def x_body(nfeat, steps, ahead, me_ref, act_hbm, proj_hbm, own_ref, *rest):
    outs, (acts, proj, total, act_sems, proj_sems) = rest[:nfeat - 1], rest[nfeat - 1:]
    rank, quarter = own_ref.shape
    depth = proj_hbm.shape[0]
    chunks = rows_of(depth, steps)
    loads = [pltpu.make_async_copy(act_hbm.at[:, c], acts.at[n], act_sems.at[n]) for n, c in enumerate(chunks)]
    proj_loads = [pltpu.make_async_copy(proj_hbm.at[c, :], proj.at[n], proj_sems.at[n]) for n, c in enumerate(chunks)]
    for n in range(ahead):
        proj_loads[n].start()
        loads[n].start()
    for n in range(steps):
        proj_loads[n].wait()
        proj_t = turn_low(proj[n])
        loads[n].wait()
        if n + ahead < steps:
            proj_loads[n + ahead].start()
            loads[n + ahead].start()
        part = turned_dot(proj_t, acts[n])
        total[...] = part if n == 0 else total[...] + part
    for j in range(nfeat):
        to = lax.rem(me_ref[0] + j, nfeat)
        value = total[:, pl.ds(pl.multiple_of(to * quarter, quarter), quarter)]
        if j == 0:
            own_ref[...] = value
        else:
            level = scale_level(jnp.max(jnp.abs(value), axis=0, keepdims=True))
            outs[j - 1][:rank, :] = to_short(value * (FULL / value_of(level)))
            outs[j - 1][rank:, :] = jnp.broadcast_to(level, (CODES, quarter)).astype(jnp.int32).astype(jnp.int16)


def project_x(me, act, proj, nfeat):
    tok, depth = act.shape
    rank = proj.shape[1]
    quarter = tok // nfeat
    steps = 7
    chunk = depth // steps
    return pl.pallas_call(
        functools.partial(x_body, nfeat, steps, 3),
        grid_spec=pltpu.PrefetchScalarGridSpec(
            num_scalar_prefetch=1,
            grid=(),
            in_specs=[HBM, HBM],
            out_specs=[VMEM] * nfeat,
            scratch_shapes=[
                pltpu.VMEM((steps, tok, chunk), BF16),
                pltpu.VMEM((steps, chunk, rank), BF16),
                pltpu.VMEM((rank, tok), F32),
                pltpu.SemaphoreType.DMA((steps,)),
                pltpu.SemaphoreType.DMA((steps,)),
            ],
        ),
        out_shape=[jax.ShapeDtypeStruct((rank, quarter), F32)]
        + [jax.ShapeDtypeStruct((rank + CODES, quarter), jnp.int16)] * (nfeat - 1),
        compiler_params=params(52),
        cost_estimate=pl.CostEstimate(flops=2 * tok * depth * rank, bytes_accessed=2 * depth * (tok + rank), transcendentals=0),
        name="project_x",
    )(me, act, proj)


def g_body(nfeat, steps, me_ref, grad_hbm, proj_hbm, starts_ref, ends_ref, own_ref, *rest):
    outs, (grads, proj, turned, grad_sems, proj_sem) = rest[:nfeat - 1], rest[nfeat - 1:]
    width, tok = own_ref.shape
    rows = rows_of(tok, steps)
    proj_load = pltpu.make_async_copy(proj_hbm, proj, proj_sem)
    proj_load.start()
    loads = [pltpu.make_async_copy(grad_hbm.at[r, :], grads.at[r, :], grad_sems.at[n]) for n, r in enumerate(rows)]
    for load in loads:
        load.start()
    proj_load.wait()
    proj_t = turn_low(proj[...])
    for n in range(0, steps, 2):
        loads[n].wait()
        loads[n + 1].wait()
        at = slice(n * tok // steps, (n + 2) * tok // steps)
        turned[:, at] = turned_dot(proj_t, grads[at, :])
    chunks = tok // LANES
    for j in range(nfeat):
        to = lax.rem(me_ref[0] + j, nfeat)
        at = pl.ds(pl.multiple_of(to * width, width), width)
        if j == 0:
            own_ref[...] = turned[at, :]
        else:
            parts = [turned[at, n * LANES:(n + 1) * LANES] for n in range(chunks)]
            peak = functools.reduce(jnp.maximum, [jnp.abs(p) for p in parts])
            level = scale_level(jnp.max(peak, axis=0, keepdims=True))
            factor = FULL / value_of(level)
            for n in range(chunks):
                outs[j - 1][n * width:(n + 1) * width, :] = to_short(parts[n] * factor)
            outs[j - 1][chunks * width:, :] = jnp.broadcast_to(level, (CODES, LANES)).astype(jnp.int32).astype(jnp.int16)


def project_g(me, grads, proj, nfeat, *after):
    tok, depth = grads.shape
    rank = proj.shape[1]
    width = rank // nfeat
    steps = 4
    short = (tok // LANES * width + CODES, LANES)
    return pl.pallas_call(
        functools.partial(g_body, nfeat, steps),
        grid_spec=pltpu.PrefetchScalarGridSpec(
            num_scalar_prefetch=1,
            grid=(),
            in_specs=[HBM, HBM] + [ANY] * len(after),
            out_specs=[VMEM] * nfeat,
            scratch_shapes=[
                pltpu.VMEM((tok, depth), BF16),
                pltpu.VMEM((depth, rank), BF16),
                pltpu.VMEM((rank, tok), F32),
                pltpu.SemaphoreType.DMA((steps,)),
                pltpu.SemaphoreType.DMA,
            ],
        ),
        out_shape=[jax.ShapeDtypeStruct((width, tok), F32)] + [jax.ShapeDtypeStruct(short, jnp.int16)] * (nfeat - 1),
        compiler_params=params(53),
        cost_estimate=pl.CostEstimate(flops=2 * tok * depth * rank, bytes_accessed=2 * depth * (tok + rank), transcendentals=0),
        name="project_g",
    )(me, grads, proj, *after)


def join_x_body(nafter, *refs):
    own_ref, others, out_ref = refs[nafter], refs[nafter + 1:-1], refs[-1]
    rows = own_ref.shape[0]
    value = own_ref[...]
    for other in others:
        scale = value_of(from_short(other[rows:, :])[0:1, :]) * (1.0 / FULL)
        value = value + from_short(other[:rows, :]) * scale
    out_ref[...] = value.astype(BF16)


def join_g_body(nafter, *refs):
    own_ref, others, out_ref = refs[nafter], refs[nafter + 1:-1], refs[-1]
    width, tok = own_ref.shape
    chunks = tok // LANES
    scales = [value_of(from_short(other[chunks * width:, :])[0:1, :]) * (1.0 / FULL) for other in others]
    for c in range(chunks):
        value = own_ref[:, c * LANES:(c + 1) * LANES]
        for other, scale in zip(others, scales):
            value = value + from_short(other[c * width:(c + 1) * width, :]) * scale
        out_ref[:, c * LANES:(c + 1) * LANES] = value.astype(BF16)


def join(body, parts, after=()):
    return pl.pallas_call(
        functools.partial(body, len(after)),
        in_specs=[ANY] * len(after) + [VMEM] * len(parts),
        out_specs=VMEM,
        out_shape=jax.ShapeDtypeStruct(parts[0].shape, BF16),
        compiler_params=params(),
        name=body.__name__,
    )(*after, *parts)


def pack_body(x_refs, *rest):
    pieces, more, out_ref = rest[:x_refs], rest[x_refs:-1], rest[-1]
    size = pieces[0].shape[1]
    for n, piece in enumerate(pieces):
        out_ref[:, n * size:(n + 1) * size] = piece[...]
    for ref in more:
        rows = ref.shape[0]
        for n in range(ref.shape[1] // size):
            out_ref[n * rows:(n + 1) * rows, x_refs * size:] = ref[:, n * size:(n + 1) * size]


def pack(pieces, more=()):
    rows, size = pieces[0].shape
    count = len(pieces) + len(more)
    return pl.pallas_call(
        functools.partial(pack_body, len(pieces)),
        in_specs=[VMEM] * count,
        out_specs=VMEM,
        out_shape=jax.ShapeDtypeStruct((rows, count * size), BF16),
        compiler_params=params(),
        name="pack",
    )(*pieces, *more)


def token_body(width, me_ref, first_ref, last_ref, out_ref):
    rank = first_ref.shape[0]
    size = last_ref.shape[1] // 2
    pieces = [first_ref[:, n * size:(n + 1) * size] for n in range(3)] + [last_ref[:, :size]]
    for source, piece in zip(sources_of(me_ref[0]), pieces):
        out_ref[:rank, pl.ds(pl.multiple_of(source * size, size), size)] = piece
    for n in range(rank // width):
        out_ref[rank:, n * size:(n + 1) * size] = last_ref[n * width:(n + 1) * width, size:]


def token_block(me, first, last, width):
    rank, size = last.shape
    return pl.pallas_call(
        functools.partial(token_body, width),
        grid_spec=pltpu.PrefetchScalarGridSpec(
            num_scalar_prefetch=1, grid=(), in_specs=[VMEM] * 2, out_specs=VMEM
        ),
        out_shape=jax.ShapeDtypeStruct((rank + width, rank // width * size // 2), BF16),
        compiler_params=params(),
        name="token_block",
    )(me, first, last)


def turn(row):
    return jnp.transpose(jnp.broadcast_to(row, (LANES, row.shape[1])))[:, 0:1]


def turn_back(column):
    return jnp.transpose(jnp.broadcast_to(column, (column.shape[0], LANES)))[0:1, :]


def norm_of(sumsq):
    return sumsq / K + 1e-06


def spread(row, lanes):
    return jnp.concatenate([row] * (lanes // row.shape[1]), axis=1)


def code_rows(rows, lanes):
    at = lax.broadcasted_iota(jnp.int32, (CODES, lanes), 0)
    tile = jnp.zeros((CODES, lanes), F32)
    for n, row in enumerate(rows):
        tile = jnp.where(at == n, spread(row, lanes), tile)
    return tile


def loads_of(corpus_hbm, corpus_ref, sems, quarters, halves):
    size = corpus_ref.shape[1]
    loads = []
    for n, quarter in enumerate(quarters):
        rows = pl.ds(pl.multiple_of(quarter * size, size), size)
        for h, here in enumerate(rows_of(corpus_ref.shape[2], halves)):
            loads.append(pltpu.make_async_copy(corpus_hbm.at[rows, here], corpus_ref.at[n, :, here], sems.at[n * halves + h]))
    return loads


def write_scores(value, sumsq, out_ref):
    passages, quarter = value.shape
    coarse = level_of(sumsq)
    fine = jnp.floor((jnp.maximum(sumsq, 1e-30) / value_of(coarse) - 1.0) * (2.0**22))
    level = scale_level(jnp.max(jnp.abs(value), axis=0, keepdims=True))
    out_ref[:passages, :] = to_short(value * (FULL / value_of(level)))
    out_ref[passages:, :] = code_rows([level, coarse, fine], quarter).astype(jnp.int32).astype(jnp.int16)


def first_body(nblk, passages, place_ref, starts_ref, ends_ref, *rest):
    blocks, corpus_hbm = rest[:nblk], rest[nblk]
    out_ref, sumsq_ref, low, held_ref, corpus_ref, tokens, grad, sems, held_sems = rest[nblk + 1:]
    me = place_ref[0]
    sources = sources_of(me)
    loads = loads_of(corpus_hbm, corpus_ref, sems, sources[3:], 1)
    later = loads_of(corpus_hbm, held_ref, held_sems, sources[1:3], 1)
    for load in loads + later:
        load.start()

    height, tok = blocks[0].shape
    rank = height - low.shape[1] // LANES
    width = height - rank
    for n in range(nblk):
        tokens[:, pl.ds(pl.multiple_of(place_ref[3 + n] * tok, tok), tok)] = blocks[n][...]
    group = 8
    window = -(-group * LONGEST // LANES) * LANES + LANES

    def step(i, carry):
        first = pl.multiple_of(i * group, group)
        base = jnp.minimum((starts_ref[first] // LANES) * LANES, nblk * tok - window)
        here = pl.ds(pl.multiple_of(base, LANES), window)
        token = base + lax.broadcasted_iota(jnp.int32, (group, window), 1)
        row = lax.broadcasted_iota(jnp.int32, (group, window), 0)
        start = jnp.zeros((group, window), jnp.int32)
        end = start
        for q in range(group):
            start = jnp.where(row == q, starts_ref[first + q], start)
            end = jnp.where(row == q, ends_ref[first + q], end)
        member = jnp.where((token >= start) & (token < end), 1.0, 0.0)
        terms = tokens[rank:, here].astype(F32)[:, None, :] * member[None, :, :]
        product = turned_dot(terms.reshape(width * group, window).astype(BF16), tokens[:rank, here])
        grad[:, pl.ds(first, group), :] = product.reshape(width, group, rank)
        return carry

    lax.fori_loop(0, passages // group, step, 0, unroll=4)
    squares = jnp.zeros((passages, LANES), F32)
    for a in range(width):
        column = grad[a]
        squares = squares + column * column
        low[:, a * LANES:(a + 1) * LANES] = column.astype(BF16)
    sumsq = jnp.sum(jnp.transpose(squares), axis=0, keepdims=True)
    sumsq_ref[...] = jnp.broadcast_to(sumsq, sumsq_ref.shape)
    norm = turn(lax.rsqrt(norm_of(sumsq)))
    for load in loads:
        load.wait()
    write_scores(norm * turned_dot(low[...], corpus_ref[0]), sumsq, out_ref)
    for load in later:
        load.wait()


def first_scores(place, starts, ends, blocks, corpus, nfeat):
    passages = starts.shape[0]
    rows, depth = corpus.shape
    quarter = rows // nfeat
    height, tok = blocks[0].shape
    nblk = len(blocks)
    return pl.pallas_call(
        functools.partial(first_body, nblk, passages),
        grid_spec=pltpu.PrefetchScalarGridSpec(
            num_scalar_prefetch=3,
            grid=(),
            in_specs=[VMEM] * nblk + [HBM],
            out_specs=[VMEM] * 4,
            scratch_shapes=[
                pltpu.VMEM((1, quarter, depth), BF16),
                pltpu.VMEM((height, nblk * tok), BF16),
                pltpu.VMEM((depth // LANES, passages, LANES), F32),
                pltpu.SemaphoreType.DMA((1,)),
                pltpu.SemaphoreType.DMA((nfeat - 2,)),
            ],
        ),
        out_shape=[
            jax.ShapeDtypeStruct((passages + CODES, quarter), jnp.int16),
            jax.ShapeDtypeStruct((8, passages), F32),
            jax.ShapeDtypeStruct((passages, depth), BF16),
            jax.ShapeDtypeStruct((nfeat - 2, quarter, depth), BF16),
        ],
        compiler_params=params(30),
        cost_estimate=pl.CostEstimate(flops=2 * passages * depth * rows, bytes_accessed=rows * depth, transcendentals=0),
        name="first_scores",
    )(place, starts, ends, *blocks, corpus)


def near_body(low_ref, sumsq_ref, held_ref, across_ref, beside_ref):
    sumsq = sumsq_ref[0:1, :]
    norm = turn(lax.rsqrt(norm_of(sumsq)))
    write_scores(norm * turned_dot(low_ref[...], held_ref[0]), sumsq, beside_ref)
    across_ref[...] = norm * turned_dot(low_ref[...], held_ref[1])


def near_scores(low, sumsq, held):
    passages, depth = low.shape
    quarter = held.shape[1]
    return pl.pallas_call(
        near_body,
        in_specs=[VMEM] * 3,
        out_specs=[VMEM] * 2,
        out_shape=[
            jax.ShapeDtypeStruct((passages, quarter), F32),
            jax.ShapeDtypeStruct((passages + CODES, quarter), jnp.int16),
        ],
        compiler_params=params(8),
        cost_estimate=pl.CostEstimate(flops=4 * passages * depth * quarter, bytes_accessed=4 * quarter * depth, transcendentals=0),
        name="near_scores",
    )(low, sumsq, held)


def own_body(me_ref, low_ref, sumsq_ref, corpus_hbm, after_ref, own_ref, held_ref, sems):
    sources = sources_of(me_ref[0])
    loads = loads_of(corpus_hbm, held_ref, sems, [sources[0], sources[3]], 1)
    for load in loads:
        load.start()
    norm = turn(lax.rsqrt(norm_of(sumsq_ref[0:1, :])))
    loads[0].wait()
    own_ref[...] = norm * turned_dot(low_ref[...], held_ref[0])
    loads[1].wait()


def own_scores(me, low, sumsq, corpus, nfeat, after):
    passages, depth = low.shape
    quarter = corpus.shape[0] // nfeat
    return pl.pallas_call(
        own_body,
        grid_spec=pltpu.PrefetchScalarGridSpec(
            num_scalar_prefetch=1,
            grid=(),
            in_specs=[VMEM] * 2 + [HBM, ANY],
            out_specs=[VMEM] * 2,
            scratch_shapes=[pltpu.SemaphoreType.DMA((2,))],
        ),
        out_shape=[jax.ShapeDtypeStruct((passages, quarter), F32), jax.ShapeDtypeStruct((2, quarter, depth), BF16)],
        compiler_params=params(30),
        cost_estimate=pl.CostEstimate(flops=2 * passages * depth * quarter, bytes_accessed=4 * quarter * depth, transcendentals=0),
        name="own_scores",
    )(me, low, sumsq, corpus, after)


def open_body(message_ref, after_ref, score_ref, sumsq_ref):
    score_ref[...], sumsq = read_scores(message_ref)
    sumsq_ref[...] = jnp.broadcast_to(sumsq, sumsq_ref.shape)


def open_scores(message, after):
    passages, size = message.shape[0] - CODES, message.shape[1]
    return pl.pallas_call(
        open_body,
        in_specs=[VMEM, ANY],
        out_specs=[VMEM] * 2,
        out_shape=[jax.ShapeDtypeStruct((passages, size), F32), jax.ShapeDtypeStruct((8, passages), F32)],
        compiler_params=params(8),
        name="open_scores",
    )(message, after)


def split3(value):
    high = value.astype(BF16)
    rest = value - high.astype(F32)
    middle = rest.astype(BF16)
    return [p.astype(F32) for p in (high, middle, (rest - middle.astype(F32)).astype(BF16))]


def pack_level(tile):
    lane = lax.broadcasted_iota(jnp.int32, tile.shape, 1)
    out = jnp.zeros(tile.shape, F32)
    for n, piece in enumerate(split3(tile)):
        out = jnp.where(lane == n, piece, out)
    return out.astype(BF16)


def unpack_level(tile):
    return jnp.broadcast_to(jnp.sum(tile.astype(F32), axis=1, keepdims=True), tile.shape)


def read_scores(ref):
    passages = ref.shape[0] - CODES
    code = from_short(ref[passages:, :])
    base = value_of(code[1:2, :passages])
    square = base + base * (code[2:3, :passages] * (1.0 / 2.0**22))
    return from_short(ref[:passages, :]) * (value_of(code[0:1, :]) * (1.0 / FULL)), square


def add_terms(terms):
    sumsq = functools.reduce(jnp.add, [square for _, square in terms])
    scale = lax.rsqrt(norm_of(sumsq))
    return functools.reduce(jnp.add, [value * turn(scale * jnp.sqrt(norm_of(square))) for value, square in terms]), sumsq


def add_body(score_ref, sumsq_ref, message_ref, out_ref):
    value, sumsq = add_terms([(score_ref[...], sumsq_ref[0:1, :]), read_scores(message_ref)])
    write_scores(value, sumsq, out_ref)


def add_scores(score, sumsq, message):
    return pl.pallas_call(
        add_body,
        in_specs=[VMEM] * 3,
        out_specs=VMEM,
        out_shape=jax.ShapeDtypeStruct(message.shape, message.dtype),
        compiler_params=params(8),
        name="add_scores",
    )(score, sumsq, message)


def half_of(value, half, owners):
    size = value.shape[0] // owners // 2
    return jnp.concatenate([value[(2 * n + half) * size:(2 * n + half + 1) * size] for n in range(owners)], axis=0)


def weight_body(owners, me_ref, owner_ref, own_ref, sumsq_ref, open_ref, open_sumsq_ref, message_ref, first_ref, second_ref):
    passages, rows = own_ref.shape
    opened = open_ref[...], open_sumsq_ref[0:1, :]
    value, _ = add_terms([(own_ref[...], sumsq_ref[0:1, :]), opened, read_scores(message_ref)])
    score = value * (2.5 / math.sqrt(K))
    owner = owner_ref[:, pl.ds(pl.multiple_of(me_ref[0] * rows, rows), rows)]
    owned = owner == lax.broadcasted_iota(jnp.int32, (passages, rows), 0)
    score = jnp.where(owned, LOW, score)
    top = jnp.max(score, axis=1, keepdims=True)
    weight = jnp.where(owned, 0.0, jnp.exp(score - top))
    total = jnp.sum(weight, axis=1, keepdims=True)
    first_ref[:passages // 2, :] = half_of(weight, 0, owners).astype(BF16)
    first_ref[passages // 2:, :] = code_rows(split3(turn_back(top)) + split3(turn_back(total)), rows).astype(BF16)
    second_ref[...] = half_of(weight, 1, owners).astype(BF16)


def weights_of(me, owner, own, sumsq, opened, message, owners):
    passages, rows = own.shape
    return pl.pallas_call(
        functools.partial(weight_body, owners),
        grid_spec=pltpu.PrefetchScalarGridSpec(
            num_scalar_prefetch=1, grid=(), in_specs=[VMEM] * 6, out_specs=[VMEM] * 2
        ),
        out_shape=[
            jax.ShapeDtypeStruct((passages // 2 + CODES, rows), BF16),
            jax.ShapeDtypeStruct((passages // 2, rows), BF16),
        ],
        compiler_params=params(8),
        cost_estimate=pl.CostEstimate(flops=8 * passages * rows, bytes_accessed=16 * passages * rows, transcendentals=passages * rows),
        name="weights",
    )(me, owner.reshape(1, -1), own, sumsq, *opened, message)


def running_stats(owners, codes, before):
    rows = 2 * (codes[0].shape[0] - CODES)
    codes = [code[code.shape[0] - CODES:, :rows].astype(F32) for code in codes]

    def columns(first):
        turned = [turn((c[first:first + 1] + c[first + 1:first + 2]) + c[first + 2:first + 3]) for c in codes]
        return [jnp.concatenate([half_of(column, half, owners) for half in range(2)], axis=0) for column in turned]

    tops, totals = columns(0), columns(3)
    if before is not None:
        tops.append(before[:, 0:1])
        totals.append(before[:, 1:2])
    top = functools.reduce(jnp.maximum, tops)
    factors = [jnp.exp(t - top) for t in tops]
    total = functools.reduce(jnp.add, [f * t for f, t in zip(factors, totals)])
    return top, total, factors


def add_sums(weights, quarters, factors, old, acc_ref):
    step = 512
    for n, (weight, quarter) in enumerate(zip(weights, quarters)):
        for at in range(0, acc_ref.shape[1], step):
            here = slice(at, at + step)
            value = factors[n] * jnp.dot(weight, quarter[:, here], preferred_element_type=F32)
            if n:
                value = acc_ref[:, here] + value
            elif old is not None:
                value = factors[-1] * old[:, here] + value
            acc_ref[:, here] = value


def stats_tile(top, total):
    lane = lax.broadcasted_iota(jnp.int32, (top.shape[0], LANES), 1)
    return jnp.where(lane == 0, top, total)


def sums_body(owners, sources, started, *rest):
    count = 2 * sources
    parts, held_ref, rest = rest[:count], rest[count], rest[count + 1:]
    before, acc_ref, stats_ref = rest[:2 * started], *rest[-2:]
    pieces = [parts[2 * n:2 * n + 2] for n in range(sources)]
    quarters = [held_ref.at[n] for n in range(sources)]
    top, total, factors = running_stats(owners, parts[::2], before[1] if before else None)
    weights = [jnp.concatenate([piece[0][:piece[1].shape[0], :], piece[1][...]], axis=0) for piece in pieces]
    add_sums(weights, quarters, factors, before[0] if before else None, acc_ref)
    stats_ref[...] = stats_tile(top, total)


def weighted_sums(owners, pieces, held, before, after=()):
    parts = [part for piece in pieces for part in piece]
    passages = 2 * parts[1].shape[0]
    _, quarter, depth = held.shape
    return pl.pallas_call(
        functools.partial(sums_body, owners, len(pieces), len(before) // 2),
        in_specs=[VMEM] * (len(parts) + 1 + len(before)) + [ANY] * len(after),
        out_specs=[VMEM] * 2,
        out_shape=[jax.ShapeDtypeStruct((passages, depth), F32), jax.ShapeDtypeStruct((passages, LANES), F32)],
        compiler_params=params(8),
        cost_estimate=pl.CostEstimate(flops=2 * passages * quarter * len(pieces) * depth, bytes_accessed=2 * quarter * depth, transcendentals=0),
        name="weighted_sums",
    )(*parts, held, *before, *after)


def last_sums_body(half, nrows, nsub, place_ref, piece_ref, held_ref, old_ref, stats_ref, *rest):
    send_ref, keep_ref, later_ref, columns_ref = rest if half == 0 else rest[:2] + (None, rest[2])
    span = send_ref.shape[1]
    depth = held_ref.shape[2]
    passages = columns_ref.shape[0]
    core = place_ref[1]
    if half == 0:
        top, total, factors = running_stats(nrows * nsub, [piece_ref], stats_ref)
        share = 1.0 / jnp.maximum(total, 1e-30)
        level = top + jnp.log(jnp.maximum(total, 1e-30))
        columns = [factors[0] * share, factors[1] * share, level]
        lane = lax.broadcasted_iota(jnp.int32, (2 * passages, LANES), 1)
        tile = jnp.where(lane == 0, columns[0], jnp.where(lane == 1, columns[1], columns[2]))
        columns_ref[...] = tile[:passages]
        later_ref[...] = tile[passages:]
    else:
        columns_ref[...] = stats_ref[...]
    starts = [x * nsub + (nsub - 1 - core) for x in range(nrows)] + [x * nsub + core for x in range(nrows)]
    rows = [pl.ds(pl.multiple_of(n * span, span), span) for n in starts]
    old_rows = [pl.ds(pl.multiple_of(half * passages + n * span, span), span) for n in starts]
    weight = jnp.concatenate([piece_ref[r, :] for r in rows], axis=0)
    columns = jnp.concatenate([columns_ref[r, :] for r in rows], axis=0)
    new_factor, old_factor, level = columns[:, 0:1], columns[:, 1:2], columns[:, 2:3]
    step = 512
    for at in range(0, depth, step):
        here = slice(at, at + step)
        old = jnp.concatenate([old_ref[r, here] for r in old_rows], axis=0)
        value = new_factor * jnp.dot(weight, held_ref[1, :, here], preferred_element_type=F32) + old_factor * old
        for x in range(nrows):
            send_ref[x, :, here] = value[x * span:(x + 1) * span].astype(BF16)
            keep_ref[x, :, here] = value[(nrows + x) * span:(nrows + x + 1) * span]
    level = jnp.broadcast_to(level, (passages, LANES))
    for x in range(nrows):
        send_ref[x, :, depth:] = pack_level(level[x * span:(x + 1) * span])
        keep_ref[x, :, depth:] = level[(nrows + x) * span:(nrows + x + 1) * span]


def last_sums(place, half, piece, held, sums, stats, nrows, nsub):
    _, quarter, depth = held.shape
    passages = sums.shape[0] // 2
    shape = (nrows, passages // (nrows * nsub), depth + LANES)
    ratios = [jax.ShapeDtypeStruct((passages, LANES), F32)] * (1 - half)
    return pl.pallas_call(
        functools.partial(last_sums_body, half, nrows, nsub),
        grid_spec=pltpu.PrefetchScalarGridSpec(
            num_scalar_prefetch=1,
            grid=(),
            in_specs=[VMEM] * 4,
            out_specs=[VMEM] * (3 - half),
            scratch_shapes=[pltpu.VMEM((passages, LANES), F32)],
        ),
        out_shape=[jax.ShapeDtypeStruct(shape, BF16), jax.ShapeDtypeStruct(shape, F32)] + ratios,
        compiler_params=params(),
        cost_estimate=pl.CostEstimate(flops=0, bytes_accessed=0, transcendentals=0),
        name="last_sums",
    )(place, piece, held, sums, stats)


def merge_shares(mine, other):
    top = jnp.maximum(mine, other)
    a, b = jnp.exp(mine - top), jnp.exp(other - top)
    share = 1.0 / (a + b)
    return a * share, b * share, top + jnp.log(a + b)


def merged(keep_ref, other_ref, a, b, tile):
    here = slice(tile * LANES, (tile + 1) * LANES)
    return keep_ref[:, here] * a + other_ref[:, here].astype(F32) * b


def merge_core_body(place_ref, keep_ref, other_ref, send_ref, next_ref):
    depth = send_ref.shape[1] - LANES
    mine = place_ref[2]
    blocks = [(keep_ref.at[at], other_ref.at[at]) for at in (1 - mine, mine)]
    shares = [merge_shares(keep[:, depth:], unpack_level(other[:, depth:])) for keep, other in blocks]
    for tile in range(depth // LANES):
        here = slice(tile * LANES, (tile + 1) * LANES)
        send_ref[:, here] = merged(*blocks[0], *shares[0][:2], tile).astype(BF16)
        next_ref[:, here] = merged(*blocks[1], *shares[1][:2], tile)
    send_ref[:, depth:] = pack_level(shares[0][2])
    next_ref[:, depth:] = shares[1][2]


def merge_core(place, keep, other):
    shape = keep.shape[1:]
    return pl.pallas_call(
        merge_core_body,
        grid_spec=pltpu.PrefetchScalarGridSpec(
            num_scalar_prefetch=1,
            grid=(),
            in_specs=[pl.BlockSpec(memory_space=pltpu.VMEM)] * 2,
            out_specs=[pl.BlockSpec(memory_space=pltpu.VMEM)] * 2,
        ),
        out_shape=[jax.ShapeDtypeStruct(shape, BF16), jax.ShapeDtypeStruct(shape, F32)],
        compiler_params=params(),
        name="merge_core",
    )(place, keep, other)


def merge_last_body(done, keep_ref, other_ref, *rest):
    out_ref = rest[-1]
    if done:
        out_ref[:done, :] = rest[0][...]
    depth = keep_ref.shape[1] - LANES
    a, b, _ = merge_shares(keep_ref[:, depth:], unpack_level(other_ref[:, depth:]))
    for tile in range(depth // LANES):
        out_ref[done:, tile * LANES:(tile + 1) * LANES] = merged(keep_ref, other_ref, a, b, tile)


def merge_last(keep, other, before):
    done = before[0].shape[0] if before else 0
    return pl.pallas_call(
        functools.partial(merge_last_body, done),
        in_specs=[VMEM] * (2 + len(before)),
        out_specs=VMEM,
        out_shape=jax.ShapeDtypeStruct((done + keep.shape[0], keep.shape[1] - LANES), F32),
        compiler_params=params(),
        name="merge_last",
    )(keep, other, *before)


def shift(value, axis, by):
    count = lax.axis_size(axis)
    return lax.ppermute(value, axis, [(i, (i + by) % count) for i in range(count)])


def scatter_parts(blocks):
    return [blocks[0]] + [shift(blocks[j], "feat", j) for j in range(1, len(blocks))]


def to_pair(value):
    return lax.ppermute(value, "feat", [(i, i ^ 1) for i in range(lax.axis_size("feat"))])


def sources_of(me):
    return [me, me ^ 1, me ^ 2, me ^ 3]


def relay_body(piece_ref, *rest):
    rest[-1][...] = piece_ref[...]


def relay(piece, *after):
    return pl.pallas_call(
        relay_body,
        in_specs=[VMEM] + [ANY] * len(after),
        out_specs=VMEM,
        out_shape=jax.ShapeDtypeStruct(piece.shape, piece.dtype),
        compiler_params=params(),
        name="relay",
    )(piece, *after)


def gather_tokens(me, g_own, g_others, piece):
    across, beside = shift(piece, "feat", 2), to_pair(piece)
    first = pack([piece, beside, across])
    g_low = join(join_g_body, [g_own] + g_others, (first,))
    last = pack([to_pair(across)], [g_low])
    width = g_low.shape[0]
    here = token_block(me, first, last, width)
    there = token_block(me, shift(first, "rows", 1), shift(last, "rows", 1), width)
    return [here, there, shift(here, "sub", 1), shift(there, "sub", 1)], [(0, 0), (1, 0), (0, 1), (1, 1)]


def fast(activations, out_grads, proj_in, proj_out, lengths, corpus, owner):
    nfeat, nrows, nsub = (lax.axis_size(a) for a in ("feat", "rows", "sub"))
    feat, row, sub = (lax.axis_index(a).astype(jnp.int32) for a in ("feat", "rows", "sub"))
    me = feat.reshape(1)
    ends = jnp.cumsum(lengths)
    starts = ends - lengths
    x_parts = project_x(me, activations, proj_in, nfeat)
    g_parts = project_g(me, out_grads, proj_out, nfeat, starts, ends)
    x_piece = join(join_x_body, scatter_parts(x_parts), g_parts[:1])
    blocks, back = gather_tokens(me, g_parts[0], scatter_parts(g_parts)[1:], x_piece)
    order = [(row ^ d) * nsub + (sub ^ c) for d, c in back]
    place = jnp.stack([feat, sub, row] + order)
    message, sumsq, low, held = first_scores(place, starts, ends, blocks, corpus, nfeat)
    across, beside = near_scores(low, sumsq, held)
    across = add_scores(across, sumsq, to_pair(message))
    own, held_far = own_scores(me, low, sumsq, corpus, nfeat, across)
    owners = nrows * nsub
    opened = open_scores(to_pair(beside), own)
    pieces = weights_of(me, owner, own, sumsq, opened, shift(across, "feat", 2), owners)
    beside, across = [to_pair(p) for p in pieces], [shift(p, "feat", 2) for p in pieces]
    sums = weighted_sums(owners, [pieces], held_far, ())
    relayed = [relay(across[0], sums[1])]
    relayed.append(relay(across[1], relayed[0]))
    last = [to_pair(p) for p in relayed]
    sums = weighted_sums(owners, [beside, across], held, sums, after=relayed[1:])
    *first, ratios = last_sums(place, 0, last[0], held_far, *sums, nrows, nsub)
    halves = [first, last_sums(place, 1, last[1], held_far, sums[0], ratios, nrows, nsub)]
    ended = [merge_core(place, keep, shift(send, "sub", 1)) for send, keep in halves]
    out = ()
    for send, keep in ended:
        out = (merge_last(keep, shift(send, "rows", 1), out),)
    return out[0]


def general(activations, out_grads, proj_in, proj_out, lengths, corpus, owner):
    tok_local = activations.shape[0]
    passages = lengths.shape[0]
    nfeat = lax.axis_size("feat")
    part_x = jnp.dot(activations, proj_in, preferred_element_type=F32)
    part_g = jnp.dot(out_grads, proj_out, preferred_element_type=F32)
    width_cols = part_g.shape[1] // nfeat
    x_low = lax.psum(part_x, "feat").astype(BF16)
    g_low = lax.psum_scatter(part_g, "feat", scatter_dimension=1, tiled=True).astype(BF16)
    ends = jnp.cumsum(lengths)
    starts = ends - lengths
    positions = lax.axis_index(("rows", "sub")) * tok_local + jnp.arange(tok_local, dtype=jnp.int32)
    member = ((positions[None, :] >= starts[:, None]) & (positions[None, :] < ends[:, None])).astype(BF16)
    scaled_member = member[None, :, :] * jnp.transpose(g_low)[:, None, :]
    partial_grad = jnp.einsum("apt,tb->pab", scaled_member, x_low, preferred_element_type=F32)
    partial_grad = partial_grad.reshape(passages, width_cols * x_low.shape[1])
    pgrad = lax.psum(partial_grad, ("rows", "sub"))
    pgrad_low = pgrad.astype(BF16)
    sumsq_part = jnp.sum(pgrad * pgrad, axis=1)
    raw_part = lax.dot_general(pgrad_low, corpus, (((1,), (1,)), ((), ())), preferred_element_type=F32)
    labels = jnp.arange(passages, dtype=jnp.int32)[:, None]
    raw, sumsq = lax.psum((raw_part, sumsq_part), "feat")
    scale = 2.5 / math.sqrt(K) * lax.rsqrt(sumsq / K + 1e-06)
    score = raw * scale[:, None]
    owned = owner[None, :] == labels
    top = lax.pmax(jnp.max(jnp.where(owned, F32(LOW), score), axis=1), ("rows", "sub"))
    weight = jnp.where(owned, F32(0.0), jnp.exp(score - top[:, None]))
    total = lax.psum(jnp.sum(weight, axis=1), ("rows", "sub"))
    span = passages // lax.axis_size(("rows", "sub"))
    summed = lax.psum_scatter(
        jnp.dot(weight.astype(BF16), corpus, preferred_element_type=F32),
        ("rows", "sub"),
        scatter_dimension=0,
        tiled=True,
    )
    own_total = lax.dynamic_slice_in_dim(total, lax.axis_index(("rows", "sub")) * span, span, 0)
    return summed / own_total[:, None]


def solution(mesh):
    small = mesh.shape["feat"] == 4 and mesh.shape["rows"] == 2 and mesh.shape["sub"] == 2
    return jax.shard_map(
        fast if small else general,
        mesh=mesh,
        in_specs=(
            P(("groups", "rows", "sub"), "feat"),
            P(("groups", "rows", "sub"), "feat"),
            P(("groups", "feat"), None),
            P(("groups", "feat"), None),
            P("groups"),
            P(("groups", "rows", "sub"), "feat"),
            P(("rows", "sub")),
        ),
        out_specs=P(("groups", "rows", "sub"), "feat"),
        check_vma=False,
    )
```
